256 devices in a mesh: blk: 8 (over y, x_hi), view: 32 (over z, x_lo, core).
Axes of the slice: x: 4 (x_hi: 2, x_lo: 2; x = x_hi * 2 + x_lo), y: 4, z: 8, core: 2. Of those that a mesh axis runs over, the one named last changes fastest.
Arguments:
- anchors: float32 [262144, 256], P(('blk', 'view')), may hold values from -0.5 to 0.5
- keys: float32 [262144, 256], P(('blk', 'view')), may hold values from -0.5 to 0.5
- matches: int32 [256, 1024], P(('blk', 'view')), may hold values from 0 to 1023, each once within a row
Outputs:
- loss: float32 [262144], P(('blk', 'view'))
- anchor_grad: float32 [262144, 256], P(('blk', 'view'))
- key_grad: float32 [262144, 256], P(('blk', 'view'))
The draws below stay inside these ranges and needn't reach their ends.
Inputs may be any that keep to these rules, and one draw needn't show every extreme that they name: Each row of matches is a permutation of 0 to 1023.
All inputs are finite; a program needn't handle non-finite values.
Results may differ from the reference program's by a relative error of at most 0.008.
Values may be sent and summed in bfloat16 or wider, within the bound.
No kernel may reach another device: no remote copies, remote signals or barrier semaphores. Data moves between devices by JAX's collectives and lax.ppermute only.
A program may use at most 64 MiB of HBM per device.

```python
import jax
import jax.numpy as jnp
from jax import lax

E = 256
ROWS = 1024
POOL = 8192
CROPS = 256
TOKENS = 262144
N_BLK = 8
N_VIEW = 32


def block_levels(key, dims, split, low, top_value):
    def one(dim, parts):
        steps = jax.random.uniform(jax.random.fold_in(jax.random.fold_in(key, 6), dim), (parts,), jnp.float32, low / len(split), top_value / len(split))
        return jnp.repeat(jnp.exp(steps), dims[dim] // parts).reshape((-1,) + (1,) * (len(dims) - dim - 1))

    gain = one(*split[0])
    for cut in split[1:]:
        gain = gain * one(*cut)
    return gain


def normal_values(own_key, shape, deviation, limit, split=(), kind=jnp.bfloat16):
    gain = block_levels(own_key, shape, split, -0.22, 0.18) if split else 1.0
    array = jax.random.normal(own_key, shape, jnp.float32) * deviation * gain
    return jnp.minimum(jnp.maximum(array, -limit), limit).astype(kind)


def setup_inputs(seed: int = 0) -> dict:
    arg_keys = jax.random.split(jax.random.key(seed), 4)
    anchors = normal_values(arg_keys[0], (TOKENS, E), 0.0625, 0.5, ((0, 256),), jnp.float32)
    keys = normal_values(arg_keys[1], (TOKENS, E), 0.0625, 0.5, ((0, 256),), jnp.float32)
    matches = jax.vmap(lambda own: jax.random.permutation(own, ROWS))(jax.random.split(arg_keys[2], CROPS)).reshape((CROPS, ROWS)).astype(jnp.int32)
    return dict(anchors=anchors, keys=keys, matches=matches)


TAU_INV = 40.0

def unit_rows(x):
    scale = lax.rsqrt(lax.optimization_barrier(jnp.sum(x * x, axis=1, keepdims=True)) + 1e-06)
    return (x * scale, scale)

def pull_back(unit, scale, grad):
    return scale * (grad - unit * lax.optimization_barrier(jnp.sum(unit * grad, axis=1, keepdims=True)))

def reference(anchors, keys, matches):
    a_unit, a_scale = unit_rows(anchors)
    k_unit, k_scale = unit_rows(keys)
    a_low = a_unit.astype(jnp.bfloat16).reshape(N_BLK, N_VIEW, ROWS, E)
    k_low = k_unit.astype(jnp.bfloat16).reshape(N_BLK, N_VIEW, ROWS, E)
    paired = matches.reshape(N_BLK, N_VIEW, ROWS)
    half = N_VIEW // 2
    offsets = (jnp.arange(N_BLK, dtype=jnp.int32) * ROWS)[:, None]

    def column(view):
        other = (view + half) % N_VIEW
        group = lax.dynamic_index_in_dim(a_low, view, 1, keepdims=False).reshape(POOL, E)
        pool = lax.dynamic_index_in_dim(k_low, other, 1, keepdims=False).reshape(POOL, E)
        index = (lax.dynamic_index_in_dim(paired, view, 1, keepdims=False) + offsets).reshape(POOL).astype(jnp.int32)
        scores = jnp.dot(group, pool.T, preferred_element_type=jnp.float32) * TAU_INV
        expo = jnp.exp(scores)
        total = lax.optimization_barrier(jnp.sum(expo, axis=1))
        weighted = jnp.dot(expo.astype(jnp.bfloat16), pool, preferred_element_type=jnp.float32)
        log_total = jnp.log(total)
        positive = jnp.take_along_axis(scores, index[:, None], axis=1)[:, 0]
        loss = log_total - positive
        matched = pool[index].astype(jnp.float32)
        anchor_dir = TAU_INV * (weighted / total[:, None] - matched)
        probs = jnp.exp(scores - log_total[:, None]).astype(jnp.bfloat16)
        key_dir = jnp.dot(probs.T, group, preferred_element_type=jnp.float32) * TAU_INV
        key_dir = key_dir.at[index].add(-TAU_INV * group.astype(jnp.float32))
        return (loss, anchor_dir, key_dir)
    loss, anchor_dir, key_dir = lax.map(column, jnp.arange(N_VIEW, dtype=jnp.int32))
    loss = loss.reshape(N_VIEW, N_BLK, ROWS).transpose(1, 0, 2).reshape(TOKENS)
    anchor_dir = anchor_dir.reshape(N_VIEW, N_BLK, ROWS, E).transpose(1, 0, 2, 3).reshape(TOKENS, E)
    owner = (jnp.arange(N_VIEW, dtype=jnp.int32) + half) % N_VIEW
    key_dir = key_dir[owner].reshape(N_VIEW, N_BLK, ROWS, E).transpose(1, 0, 2, 3).reshape(TOKENS, E)
    return (loss, pull_back(a_unit, a_scale, anchor_dir), pull_back(k_unit, k_scale, key_dir))
```

```python
import math

import jax
import jax.numpy as jnp
from jax import lax
from jax.experimental import pallas as pl
from jax.experimental.pallas import tpu as pltpu
from jax.sharding import PartitionSpec as P

TAU_INV = 40.0
EXP2_SCALE = TAU_INV * math.log2(math.e)
TILE = 256


def view_half(block):
    count = lax.axis_size("view")
    route = [(i, (i + count // 2) % count) for i in range(count)]
    return lax.ppermute(block, "view", route)


def x_swap(block):
    return lax.ppermute(block, "blk", [(i, i ^ 1) for i in range(lax.axis_size("blk"))])


def y_shift(block, distance):
    count = lax.axis_size("blk")
    half = count // 2
    route = [(i, (i // 2 + distance) % half * 2 + i % 2) for i in range(count)]
    return lax.ppermute(block, "blk", route)


def unit_rows(x):
    scale = lax.rsqrt(jnp.sum(x * x, axis=1, keepdims=True) + 1e-06)
    return (x * scale, scale)


def pull_back(unit, scale, grad):
    return scale * (grad - unit * jnp.sum(unit * grad, axis=1, keepdims=True))


def dot_cols(left, right):
    return lax.dot_general(
        left, right, (((0,), (0,)), ((), ())), preferred_element_type=jnp.float32
    )


def expo_kernel(a_ref, *refs):
    n = (len(refs) - 2) // 2
    keys, expos, total_ref, weighted_ref = refs[:n], refs[n : 2 * n], refs[-2], refs[-1]
    a = a_ref[...]
    lanes = jnp.zeros((a.shape[0], 128), jnp.float32)
    weighted = jnp.zeros(weighted_ref.shape, jnp.float32)
    for k_ref, e_ref in zip(keys, expos):
        k = k_ref[...]
        scores = lax.dot_general(
            a, k, (((1,), (1,)), ((), ())), preferred_element_type=jnp.float32
        )
        expo = jnp.exp2(scores * EXP2_SCALE)
        for c in range(0, expo.shape[1], 128):
            lanes += expo[:, c : c + 128]
        low = expo.astype(jnp.bfloat16)
        e_ref[...] = low
        weighted += jnp.dot(low, k, preferred_element_type=jnp.float32)
    total_ref[...] = jnp.broadcast_to(jnp.sum(lanes.T, axis=0, keepdims=True), total_ref.shape)
    weighted_ref[...] = weighted


def expo_pass(a, keys):
    rows, width = a.shape
    n = len(keys)
    pool = rows * n
    whole = pl.BlockSpec((rows, width), lambda i: (0, 0))
    tile_e = pl.BlockSpec((TILE, rows), lambda i: (i, 0))
    out = pl.pallas_call(
        expo_kernel,
        grid=(rows // TILE,),
        in_specs=[pl.BlockSpec((TILE, width), lambda i: (i, 0))] + [whole] * n,
        out_specs=[tile_e] * n
        + [
            pl.BlockSpec((8, TILE), lambda i: (0, i)),
            pl.BlockSpec((TILE, width), lambda i: (i, 0)),
        ],
        out_shape=[jax.ShapeDtypeStruct((rows, rows), jnp.bfloat16)] * n
        + [
            jax.ShapeDtypeStruct((8, rows), jnp.float32),
            jax.ShapeDtypeStruct((rows, width), jnp.float32),
        ],
        compiler_params=pltpu.CompilerParams(vmem_limit_bytes=40 * 2**20),
        cost_estimate=pl.CostEstimate(
            flops=4 * rows * pool * width,
            bytes_accessed=2 * rows * pool + 2 * pool * width,
            transcendentals=rows * pool,
        ),
        name="expo_pass",
    )(a, *keys)
    return out[:n], out[n][0], out[n + 1]


def key_kernel(e0_ref, e1_ref, b0_ref, b1_ref, out_ref):
    grad = dot_cols(e0_ref[...], b0_ref[...]) + dot_cols(e1_ref[...], b1_ref[...])
    out_ref[...] = (TAU_INV * grad).astype(out_ref.dtype)


def key_pass(e0, e1, b0, b1, dtype):
    rows, width = b0.shape
    tile = pl.BlockSpec((rows, TILE), lambda i: (0, i))
    whole = pl.BlockSpec((rows, width), lambda i: (0, 0))
    return pl.pallas_call(
        key_kernel,
        grid=(rows // TILE,),
        in_specs=[tile, tile, whole, whole],
        out_specs=pl.BlockSpec((TILE, width), lambda i: (i, 0)),
        out_shape=jax.ShapeDtypeStruct((rows, width), dtype),
        compiler_params=pltpu.CompilerParams(vmem_limit_bytes=40 * 2**20),
        cost_estimate=pl.CostEstimate(
            flops=4 * rows * rows * width, bytes_accessed=4 * rows * rows, transcendentals=0
        ),
        name="key_pass",
    )(e0, e1, b0, b1)


def per_device(anchors, keys, matches):
    rows, width_e = anchors.shape
    half = lax.axis_size("blk") // 2
    a_unit, a_scale = unit_rows(anchors)
    a_low = a_unit.astype(jnp.bfloat16)
    mine = view_half(a_low)
    paired = view_half(matches)
    k_unit, k_scale = unit_rows(keys)
    k_low = k_unit.astype(jnp.bfloat16)
    pool = [k_low] + [y_shift(k_low, d) for d in range(1, half)]
    other = x_swap(mine)
    onehot = (paired[0][:, None] == jnp.arange(rows, dtype=jnp.int32)[None, :]).astype(
        jnp.bfloat16
    )
    matched = jnp.dot(onehot, k_low, preferred_element_type=jnp.float32)
    positive = jnp.sum(mine.astype(jnp.float32) * matched, axis=1) * TAU_INV
    key_own = -TAU_INV * dot_cols(onehot, mine)
    expo_m, total_m, weighted_m = expo_pass(mine, pool)
    expo_o, total_o, weighted_o = expo_pass(other, pool)
    received = x_swap(jnp.stack([total_o, total_m]))
    total_m = total_m + received[0]
    total_o = total_o + received[1]
    weighted_m = weighted_m + x_swap(weighted_o.astype(jnp.bfloat16)).astype(jnp.float32)
    b_m = (mine.astype(jnp.float32) / total_m[:, None]).astype(jnp.bfloat16)
    b_o = (other.astype(jnp.float32) / total_o[:, None]).astype(jnp.bfloat16)
    parts = []
    for d in (2, 1, 3):
        part = key_pass(expo_m[d], expo_o[d], b_m, b_o, jnp.bfloat16)
        parts.append(y_shift(part, half - d))
    key_dir = key_own + key_pass(expo_m[0], expo_o[0], b_m, b_o, jnp.float32)
    for part in parts:
        key_dir = key_dir + part.astype(jnp.float32)
    loss = view_half((jnp.log(total_m) - positive)[None, :])[0]
    anchor_dir = TAU_INV * (weighted_m / total_m[:, None] - matched)
    anchor_dir = view_half(anchor_dir.astype(jnp.bfloat16)).astype(jnp.float32)
    return (loss, pull_back(a_unit, a_scale, anchor_dir), pull_back(k_unit, k_scale, key_dir))


def solution(mesh):
    placed = (P(("blk", "view"), None), P(("blk", "view"), None), P(("blk", "view"), None))
    return jax.shard_map(
        per_device,
        mesh=mesh,
        in_specs=placed,
        out_specs=(P(("blk", "view")), P(("blk", "view"), None), P(("blk", "view"), None)),
        check_vma=False,
    )
```

```python
import functools
import math

import jax
import jax.numpy as jnp
from jax import lax
from jax.experimental import pallas as pl
from jax.experimental.pallas import tpu as pltpu
from jax.sharding import PartitionSpec as P

TAU_INV = 40.0
EXP2_SCALE = TAU_INV * math.log2(math.e)
STRIP = 256
LINE = 256
EXTRA = 16
TURN_AFTER = 2
ANCHOR_SIDE = 2
KEY_SIDE = (7, 6, 1)
VMEM = pl.BlockSpec(memory_space=pltpu.VMEM)
ANY = pl.BlockSpec(memory_space=pl.ANY)
PARAMS = pltpu.CompilerParams(vmem_limit_bytes=16 * 2**20)
HEAVY = pl.CostEstimate(flops=2**32, bytes_accessed=2**20, transcendentals=0)
LIGHT = pl.CostEstimate(flops=1024, bytes_accessed=1024, transcendentals=0)


def ordered(kernel, inputs, after):
    def body(*refs):
        kernel(*refs[:inputs], *refs[inputs + len(after) :])

    return body


def view_half(block):
    count = lax.axis_size("view")
    route = [(i, (i + count // 2) % count) for i in range(count)]
    return lax.ppermute(block, "view", route)


def swap(block, mask):
    return lax.ppermute(block, "blk", [(i, i ^ mask) for i in range(lax.axis_size("blk"))])


def dot_rows(left, right):
    return lax.dot_general(
        left, right, (((1,), (1,)), ((), ())), preferred_element_type=jnp.float32
    )


def dot_cols(left, right):
    return lax.dot_general(
        left, right, (((0,), (0,)), ((), ())), preferred_element_type=jnp.float32
    )


def as_row(column):
    wide = jnp.broadcast_to(column, (column.shape[0], 128))
    return wide.T[0:1]


def as_column(row):
    return jnp.broadcast_to(row, (128, row.shape[1])).T[:, 0:1]


def wide(row):
    width = LINE
    return jnp.concatenate([row[:, c : c + width] for c in range(0, row.shape[1], width)], axis=0)


def flat(block):
    return jnp.concatenate([block[i : i + 1] for i in range(block.shape[0])], axis=1)


def stow(ref, start, row):
    rest = wide(row)
    parts = []
    for _ in range(3):
        part = rest.astype(jnp.bfloat16).astype(jnp.float32)
        parts.append(part)
        rest = rest - part
    parts.append(jnp.zeros((EXTRA - 3 * rest.shape[0], LINE), jnp.float32))
    ref[start : start + EXTRA, :] = jnp.concatenate(parts, axis=0).astype(jnp.bfloat16)


def fetch(ref, start, count):
    block = ref[start : start + EXTRA, :].astype(jnp.float32)
    total = block[0:count] + block[count : 2 * count] + block[2 * count : 3 * count]
    return flat(total)


def unit(x):
    return x * lax.rsqrt(jnp.sum(x * x, axis=1, keepdims=True) + 1e-06)


def unit_kernel(x_ref, low_ref):
    low_ref[...] = unit(x_ref[...]).astype(low_ref.dtype)


def unit_match_kernel(x_ref, match_ref, low_ref):
    rows = x_ref.shape[0]
    low_ref[0:rows, :] = unit(x_ref[...]).astype(low_ref.dtype)
    match = match_ref[...]
    high = wide(lax.shift_right_logical(match, 5).astype(jnp.float32))
    low = wide((match & 31).astype(jnp.float32))
    fill = jnp.zeros((EXTRA - 2 * low.shape[0], LINE), jnp.float32)
    low_ref[rows : rows + EXTRA, :] = jnp.concatenate([high, low, fill], axis=0).astype(low_ref.dtype)


def unit_pass(x, start, rows, match=None):
    width = x.shape[1]
    extra = 0 if match is None else EXTRA
    specs = [pl.BlockSpec((rows, width), lambda i: (start // rows, 0))]
    if match is not None:
        specs.append(pl.BlockSpec((1, rows), lambda i: (0, start // rows)))
    return pl.pallas_call(
        unit_kernel if match is None else unit_match_kernel,
        grid=(1,),
        in_specs=specs,
        out_specs=pl.BlockSpec((rows + extra, width), lambda i: (0, 0)),
        out_shape=jax.ShapeDtypeStruct((rows + extra, width), jnp.bfloat16),
        compiler_params=PARAMS,
        cost_estimate=LIGHT,
        name="unit_pass",
    )(*([x] if match is None else [x, match]))


def match_kernel(k_ref, *refs):
    n = len(refs) - 3
    anchors, matched_ref, positive_ref, own_ref = refs[:n], *refs[n:]
    rows = k_ref.shape[0]
    part = rows // n
    count = part // LINE
    own = jnp.zeros(own_ref.shape, jnp.float32)
    for h, a_ref in enumerate(anchors):
        span = slice(h * part, (h + 1) * part)
        code = a_ref[part : part + EXTRA, :].astype(jnp.float32)
        match = flat(code[0:count] * 32.0 + code[count : 2 * count]).astype(jnp.int32)
        index = lax.broadcasted_iota(jnp.int32, (rows, part), 0)
        hot = (index == match).astype(jnp.float32).astype(jnp.bfloat16)
        a = a_ref[0:part, :]
        own += jnp.dot(hot, a, preferred_element_type=jnp.float32)
        matched = dot_cols(hot, k_ref[...])
        matched_ref[span, :] = matched
        score = jnp.sum(a.astype(jnp.float32) * matched, axis=1, keepdims=True)
        positive_ref[:, span] = as_row(score * TAU_INV)
    own_ref[...] = -TAU_INV * own


def match_pass(keys, anchors):
    rows, width = keys.shape
    return pl.pallas_call(
        match_kernel,
        in_specs=[VMEM] * (1 + len(anchors)),
        out_specs=[VMEM] * 3,
        out_shape=[
            jax.ShapeDtypeStruct((rows, width), jnp.float32),
            jax.ShapeDtypeStruct((1, rows), jnp.float32),
            jax.ShapeDtypeStruct((rows, width), jnp.float32),
        ],
        compiler_params=PARAMS,
        cost_estimate=HEAVY,
        name="match_pass",
    )(keys, *anchors)


def expo_body(a_ref, keys, expos):
    rows = a_ref.shape[0] - EXTRA
    a = a_ref[0:rows, :]
    lanes = jnp.zeros((rows, 128), jnp.float32)
    weighted = jnp.zeros((rows, a.shape[1]), jnp.float32)
    for k_ref, e_ref in zip(keys, expos):
        for j in range(0, k_ref.shape[0], STRIP):
            k = k_ref[j : j + STRIP, :]
            expo = jnp.exp2(dot_rows(a, k) * EXP2_SCALE)
            for c in range(0, STRIP, 128):
                lanes += expo[:, c : c + 128]
            low = expo.astype(jnp.bfloat16)
            e_ref[:, j : j + STRIP] = low
            weighted += jnp.dot(low, k, preferred_element_type=jnp.float32)
    return jnp.sum(lanes.T, axis=0, keepdims=True), weighted


def expo_mine_kernel(a_ref, *refs):
    n = (len(refs) - 2) // 2
    total, weighted = expo_body(a_ref, refs[:n], refs[n : 2 * n])
    refs[-2][...] = total
    refs[-1][...] = weighted


def expo_other_kernel(a_ref, mine_ref, *refs):
    n = (len(refs) - 2) // 2
    total, weighted = expo_body(a_ref, refs[:n], refs[n : 2 * n])
    rows = weighted.shape[0]
    mine = mine_ref[...]
    refs[-2][0:1, :] = total
    refs[-2][1:2, :] = mine
    refs[-1][0:rows, :] = weighted.astype(jnp.bfloat16)
    stow(refs[-1], rows, jnp.concatenate([total, mine], axis=1))


def expo_pass(a, keys, mine=None):
    rows, width = a.shape[0] - EXTRA, a.shape[1]
    n = len(keys)
    if mine is None:
        kernel, extra = expo_mine_kernel, []
        tail = [
            jax.ShapeDtypeStruct((1, rows), jnp.float32),
            jax.ShapeDtypeStruct((rows, width), jnp.float32),
        ]
    else:
        kernel, extra = expo_other_kernel, [mine]
        tail = [
            jax.ShapeDtypeStruct((2, rows), jnp.float32),
            jax.ShapeDtypeStruct((rows + EXTRA, width), jnp.bfloat16),
        ]
    out = pl.pallas_call(
        kernel,
        in_specs=[VMEM] * (1 + len(extra) + n),
        out_specs=[VMEM] * (n + 2),
        out_shape=[jax.ShapeDtypeStruct((rows, k.shape[0]), jnp.bfloat16) for k in keys] + tail,
        compiler_params=PARAMS,
        cost_estimate=LIGHT,
        name="expo_pass",
    )(a, *extra, *keys)
    return out[:n], out[n], out[n + 1]


def turn(weighted, sent, total, matched):
    weighted = weighted + sent.astype(jnp.float32)
    return (TAU_INV * (weighted * as_column(1.0 / total) - matched)).astype(jnp.bfloat16)


def turn_first_kernel(weighted_ref, sent_ref, own_ref, matched_ref, out_ref, mine_ref, other_ref):
    rows = weighted_ref.shape[0]
    got = fetch(sent_ref, rows, 2 * rows // LINE)
    mine = own_ref[1:2, :] + got[:, 0:rows]
    mine_ref[...] = mine
    other_ref[...] = own_ref[0:1, :] + got[:, rows : 2 * rows]
    out_ref[...] = turn(weighted_ref[...], sent_ref[0:rows, :], mine, matched_ref[0:rows, :])


def turn_first(weighted, sent, own, matched):
    rows, width = weighted.shape
    return pl.pallas_call(
        turn_first_kernel,
        in_specs=[VMEM] * 4,
        out_specs=[VMEM] * 3,
        out_shape=[jax.ShapeDtypeStruct((rows, width), jnp.bfloat16)]
        + [jax.ShapeDtypeStruct((1, rows), jnp.float32)] * 2,
        compiler_params=PARAMS,
        cost_estimate=LIGHT,
        name="turn_first",
    )(weighted, sent, own, matched)


def turn_last_kernel(weighted_ref, sent_ref, first_ref, last_ref, matched_ref, positive_ref, out_ref):
    rows = weighted_ref.shape[0]
    last = last_ref[...]
    out_ref[0:rows, :] = turn(
        weighted_ref[...], sent_ref[0:rows, :], last, matched_ref[rows : 2 * rows, :]
    )
    stow(
        out_ref,
        rows,
        jnp.log(jnp.concatenate([first_ref[...], last], axis=1)) - positive_ref[...],
    )


def turn_last(weighted, sent, first, last, matched, positive, after):
    rows, width = weighted.shape
    return pl.pallas_call(
        ordered(turn_last_kernel, 6, after),
        in_specs=[VMEM] * 6 + [ANY] * len(after),
        out_specs=VMEM,
        out_shape=jax.ShapeDtypeStruct((rows + EXTRA, width), jnp.bfloat16),
        compiler_params=PARAMS,
        cost_estimate=LIGHT,
        name="turn_last",
    )(weighted, sent, first, last, matched, positive, *after)


def share_kernel(*refs):
    anchors, (mine_ref, other_ref, own_ref, got_ref) = refs[:4], refs[4:8]
    outs, last_ref = refs[8:12], refs[12]
    last = own_ref[1:2, :] + got_ref[0:1, :]
    last_ref[...] = last
    totals = [mine_ref[...], last, other_ref[...], own_ref[0:1, :] + got_ref[1:2, :]]
    for a_ref, total, out_ref in zip(anchors, totals, outs):
        a = a_ref[0 : out_ref.shape[0], :].astype(jnp.float32)
        out_ref[...] = (a * as_column(1.0 / total)).astype(out_ref.dtype)


def share_pass(anchors, mine, other, own, got):
    rows, width = anchors[0].shape[0] - EXTRA, anchors[0].shape[1]
    out = pl.pallas_call(
        share_kernel,
        in_specs=[VMEM] * 8,
        out_specs=[VMEM] * 5,
        out_shape=[jax.ShapeDtypeStruct((rows, width), jnp.bfloat16)] * 4
        + [jax.ShapeDtypeStruct((1, rows), jnp.float32)],
        compiler_params=PARAMS,
        cost_estimate=LIGHT,
        name="share_pass",
    )(*anchors, mine, other, own, got)
    return out[:4], out[4]


def key_kernel(*refs):
    n = len(refs) // 2
    grad = dot_cols(refs[0][...], refs[n][...])
    for e_ref, b_ref in zip(refs[1:n], refs[n + 1 : 2 * n]):
        grad += dot_cols(e_ref[...], b_ref[...])
    refs[-1][...] = (TAU_INV * grad).astype(refs[-1].dtype)


def key_pass(expos, shares, dtype, after=(), cost=LIGHT):
    rows, width = expos[0].shape[1], shares[0].shape[1]
    return pl.pallas_call(
        ordered(key_kernel, 2 * len(expos), after),
        in_specs=[VMEM] * (2 * len(expos)) + [ANY] * len(after),
        out_specs=VMEM,
        out_shape=jax.ShapeDtypeStruct((rows, width), dtype),
        compiler_params=PARAMS,
        cost_estimate=cost,
        name="key_pass",
    )(*expos, *shares, *after)


def pull_kernel(x_ref, *refs):
    x = x_ref[...]
    scale = lax.rsqrt(jnp.sum(x * x, axis=1, keepdims=True) + 1e-06)
    unit = x * scale
    grad = refs[0][...].astype(jnp.float32)
    for ref in refs[1:-1]:
        grad += ref[...].astype(jnp.float32)
    refs[-1][...] = scale * (grad - unit * jnp.sum(unit * grad, axis=1, keepdims=True))


def pull_rest_kernel(x_ref, grad_ref, done_ref, out_ref, loss_ref):
    del done_ref
    rows = x_ref.shape[0]
    pull_kernel(x_ref, grad_ref.at[0:rows, :], out_ref)
    loss_ref[...] = fetch(grad_ref, rows, 2 * rows // LINE)


def pull_pass(x, terms, rows, after=(), cost=LIGHT):
    tile = pl.BlockSpec((STRIP, x.shape[1]), lambda i: (i, 0))
    return pl.pallas_call(
        ordered(pull_kernel, 1 + len(terms), after),
        grid=(rows // STRIP,),
        in_specs=[tile] * (1 + len(terms)) + [ANY] * len(after),
        out_specs=tile,
        out_shape=jax.ShapeDtypeStruct(x.shape, jnp.float32),
        compiler_params=PARAMS,
        cost_estimate=cost,
        name="pull_pass",
    )(x, *terms, *after)


def pull_rest(x, term, done):
    rows = x.shape[0] // 2
    moved = pl.BlockSpec((rows, x.shape[1]), lambda i: (1, 0))
    return pl.pallas_call(
        pull_rest_kernel,
        grid=(1,),
        in_specs=[
            moved,
            pl.BlockSpec(term.shape, lambda i: (0, 0)),
            ANY,
        ],
        out_specs=[moved, pl.BlockSpec((1, 2 * rows), lambda i: (0, 0))],
        out_shape=[
            jax.ShapeDtypeStruct(x.shape, jnp.float32),
            jax.ShapeDtypeStruct((1, 2 * rows), jnp.float32),
        ],
        input_output_aliases={2: 0},
        compiler_params=PARAMS,
        cost_estimate=HEAVY,
        name="pull_rest",
    )(x, term, done)


def per_device(anchors, keys, matches):
    rows = anchors.shape[0]
    part = rows // 2
    a_low = [unit_pass(anchors, s, part, matches) for s in (0, part)]
    a_low, keys = lax.optimization_barrier((a_low, keys))
    mine = [view_half(a) for a in a_low]
    k_low = unit_pass(keys, 0, rows)
    pool = [k_low] + [swap(k_low, d) for d in KEY_SIDE]
    other = [swap(a, ANCHOR_SIDE) for a in mine]
    matched, positive, key_own = match_pass(k_low, mine)
    matched, pool = lax.optimization_barrier((matched, pool))
    done_m, done_o, back = [], [], []
    for a, o in zip(mine, other):
        if done_o:
            a, done_o[-1] = lax.optimization_barrier((a, done_o[-1]))
        done_m.append(expo_pass(a, pool))
        o, done_m[-1] = lax.optimization_barrier((o, done_m[-1]))
        done_o.append(expo_pass(o, pool, done_m[-1][1]))
        back.append(swap(done_o[-1][2], ANCHOR_SIDE))
    expos = [d[0] for d in done_m + done_o]
    got = swap(done_o[1][1], ANCHOR_SIDE)
    turn_0, mine_0, other_0 = turn_first(done_m[0][2], back[0], done_o[0][1], matched)
    turned_0 = view_half(turn_0)
    shares, mine_1 = share_pass(mine + other, mine_0, other_0, done_o[1][1], got)
    parts, sent = [], []
    for d in (1, 2, 3):
        parts.append(key_pass([e[d] for e in expos], shares, jnp.bfloat16, parts[-1:]))
        sent.append(swap(parts[-1], KEY_SIDE[d - 1]))
    turn_1 = turn_last(done_m[1][2], back[1], mine_0, mine_1, matched, positive, parts[TURN_AFTER:])
    turned_1 = view_half(turn_1)
    key_0 = key_pass([e[0] for e in expos], shares, jnp.float32, [turn_1], HEAVY)
    anchor_grad = pull_pass(anchors, [turned_0], part, [key_0])
    anchor_grad, loss = pull_rest(anchors, turned_1, anchor_grad)
    key_grad = pull_pass(keys, [key_own, key_0, *sent], rows, [anchor_grad])
    return (loss.reshape(rows), anchor_grad, key_grad)


def solution(mesh):
    placed = (P(("blk", "view"), None), P(("blk", "view"), None), P(("blk", "view"), None))
    return jax.shard_map(
        per_device,
        mesh=mesh,
        in_specs=placed,
        out_specs=(P(("blk", "view")), P(("blk", "view"), None), P(("blk", "view"), None)),
        check_vma=False,
    )
```

```python
import functools
import math

import jax
import jax.numpy as jnp
from jax import lax
from jax.experimental import pallas as pl
from jax.experimental.pallas import tpu as pltpu
from jax.sharding import PartitionSpec as P

TAU_INV = 40.0
EXP2_SCALE = TAU_INV * math.log2(math.e)
STRIP = 256
LINE = 256
EXTRA = 16
ANCHOR_SIDE = 1
KEY_SIDE = (2, 6, 4)
VMEM = pl.BlockSpec(memory_space=pltpu.VMEM)
ANY = pl.BlockSpec(memory_space=pl.ANY)
HBM = pl.BlockSpec(memory_space=pltpu.HBM)
PARAMS = pltpu.CompilerParams(vmem_limit_bytes=16 * 2**20)
HEAVY = pl.CostEstimate(flops=2**32, bytes_accessed=2**20, transcendentals=0)
FIRST = pl.CostEstimate(flops=2**32, bytes_accessed=2**20, transcendentals=0)
LIGHT = pl.CostEstimate(flops=1024, bytes_accessed=1024, transcendentals=0)


def ordered(kernel, inputs, after):
    def body(*refs):
        kernel(*refs[:inputs], *refs[inputs + len(after) :])

    return body


def view_half(block):
    count = lax.axis_size("view")
    route = [(i, (i + count // 2) % count) for i in range(count)]
    return lax.ppermute(block, "view", route)


def swap(block, mask):
    return lax.ppermute(block, "blk", [(i, i ^ mask) for i in range(lax.axis_size("blk"))])


def dot_rows(left, right):
    return lax.dot_general(
        left, right, (((1,), (1,)), ((), ())), preferred_element_type=jnp.float32
    )


def dot_cols(left, right):
    return lax.dot_general(
        left, right, (((0,), (0,)), ((), ())), preferred_element_type=jnp.float32
    )


def as_row(column):
    wide = jnp.broadcast_to(column, (column.shape[0], 128))
    return wide.T[0:1]


def as_column(row):
    return jnp.broadcast_to(row, (128, row.shape[1])).T[:, 0:1]


def wide(row):
    width = LINE
    return jnp.concatenate([row[:, c : c + width] for c in range(0, row.shape[1], width)], axis=0)


def flat(block):
    return jnp.concatenate([block[i : i + 1] for i in range(block.shape[0])], axis=1)


def stow(ref, start, row):
    rest = wide(row)
    parts = []
    for _ in range(3):
        part = rest.astype(jnp.bfloat16).astype(jnp.float32)
        parts.append(part)
        rest = rest - part
    parts.append(jnp.zeros((EXTRA - 3 * rest.shape[0], LINE), jnp.float32))
    ref[start : start + EXTRA, :] = jnp.concatenate(parts, axis=0).astype(jnp.bfloat16)


def fetch(ref, start, count):
    block = ref[start : start + EXTRA, :].astype(jnp.float32)
    total = block[0:count] + block[count : 2 * count] + block[2 * count : 3 * count]
    return flat(total)


def unit(x):
    return x * lax.rsqrt(jnp.sum(x * x, axis=1, keepdims=True) + 1e-06)


def unit_kernel(start, x_hbm, low_ref, x_ref, sem):
    rows = x_ref.shape[0]
    load = pltpu.make_async_copy(x_hbm.at[pl.ds(start, rows)], x_ref, sem)
    load.start()
    load.wait()
    low_ref[0:rows, :] = unit(x_ref[...]).astype(low_ref.dtype)


def unit_match_kernel(start, x_hbm, match_ref, low_ref, x_ref, sem):
    rows = x_ref.shape[0]
    load = pltpu.make_async_copy(x_hbm.at[pl.ds(start, rows)], x_ref, sem)
    load.start()
    match = match_ref[...]
    high = wide(lax.shift_right_logical(match, 5).astype(jnp.float32))
    low = wide((match & 31).astype(jnp.float32))
    fill = jnp.zeros((EXTRA - 2 * low.shape[0], LINE), jnp.float32)
    low_ref[rows : rows + EXTRA, :] = jnp.concatenate([high, low, fill], axis=0).astype(low_ref.dtype)
    load.wait()
    low_ref[0:rows, :] = unit(x_ref[...]).astype(low_ref.dtype)


def unit_pass(x, start, rows, match=None, after=()):
    width = x.shape[1]
    kernel = functools.partial(unit_kernel if match is None else unit_match_kernel, start)
    given = [x] if match is None else [x, match]
    extra = 0 if match is None else EXTRA
    return pl.pallas_call(
        ordered(kernel, len(given), after),
        in_specs=[HBM] + [VMEM] * (len(given) - 1) + [ANY] * len(after),
        out_specs=VMEM,
        out_shape=jax.ShapeDtypeStruct((rows + extra, width), jnp.bfloat16),
        scratch_shapes=[pltpu.VMEM((rows, width), jnp.float32), pltpu.SemaphoreType.DMA],
        compiler_params=PARAMS,
        cost_estimate=LIGHT,
        name="unit_pass",
    )(*given, *after)


def match_kernel(start, k_ref, a_ref, code_ref, matched_ref, positive_ref, own_ref):
    rows = k_ref.shape[0]
    part = matched_ref.shape[0]
    count = rows // LINE
    code = code_ref[part : part + EXTRA, :].astype(jnp.float32)
    match = flat(code[0:count] * 32.0 + code[count : 2 * count]).astype(jnp.int32)
    index = lax.broadcasted_iota(jnp.int32, (rows, part), 0)
    hot = (index == match[:, start : start + part]).astype(jnp.float32).astype(jnp.bfloat16)
    a = a_ref[0:part, :]
    matched = dot_cols(hot, k_ref[...])
    matched_ref[...] = matched
    score = jnp.sum(a.astype(jnp.float32) * matched, axis=1, keepdims=True)
    positive_ref[...] = as_row(score * TAU_INV)
    own_ref[...] = -TAU_INV * jnp.dot(hot, a, preferred_element_type=jnp.float32)


def match_pass(keys, anchors, code, start, after=(), cost=LIGHT):
    rows, width = keys.shape
    part = rows // 2
    return pl.pallas_call(
        ordered(functools.partial(match_kernel, start), 3, after),
        in_specs=[VMEM] * 3 + [ANY] * len(after),
        out_specs=[VMEM] * 3,
        out_shape=[
            jax.ShapeDtypeStruct((part, width), jnp.float32),
            jax.ShapeDtypeStruct((1, part), jnp.float32),
            jax.ShapeDtypeStruct((rows, width), jnp.float32),
        ],
        compiler_params=PARAMS,
        cost_estimate=cost,
        name="match_pass",
    )(keys, anchors, code, *after)


def expo_body(a_ref, keys, expos):
    rows = expos[0].shape[0]
    a = a_ref[0:rows, :]
    lanes = jnp.zeros((rows, 128), jnp.float32)
    weighted = jnp.zeros((rows, a.shape[1]), jnp.float32)
    for k_ref, e_ref in zip(keys, expos):
        for j in range(0, k_ref.shape[0], STRIP):
            k = k_ref[j : j + STRIP, :]
            expo = jnp.exp2(dot_rows(a, k) * EXP2_SCALE)
            for c in range(0, STRIP, 128):
                lanes += expo[:, c : c + 128]
            low = expo.astype(jnp.bfloat16)
            e_ref[:, j : j + STRIP] = low
            weighted += jnp.dot(low, k, preferred_element_type=jnp.float32)
    return jnp.sum(lanes.T, axis=0, keepdims=True), weighted


def expo_mine_kernel(a_ref, *refs):
    n = (len(refs) - 2) // 2
    total, weighted = expo_body(a_ref, refs[:n], refs[n : 2 * n])
    refs[-2][...] = total
    refs[-1][...] = weighted


def expo_rest_kernel(k_ref, *refs):
    n = len(refs) // 6
    for i in range(n):
        a_ref, total_ref, weighted_ref = refs[i], refs[n + i], refs[2 * n + i]
        total, weighted = expo_body(a_ref, [k_ref], [refs[3 * n + i]])
        refs[4 * n + i][...] = total_ref[...] + total
        refs[5 * n + i][...] = weighted_ref[...] + weighted


def expo_rest(key, anchors, totals, weighted):
    rows = weighted[0].shape[0]
    n = len(anchors)
    out = pl.pallas_call(
        expo_rest_kernel,
        in_specs=[VMEM] * (1 + 3 * n),
        out_specs=[VMEM] * (3 * n),
        out_shape=[jax.ShapeDtypeStruct((rows, key.shape[0]), jnp.bfloat16)] * n
        + [jax.ShapeDtypeStruct(totals[0].shape, jnp.float32)] * n
        + [jax.ShapeDtypeStruct(weighted[0].shape, jnp.float32)] * n,
        compiler_params=PARAMS,
        cost_estimate=LIGHT,
        name="expo_rest",
    )(key, *anchors, *totals, *weighted)
    return out[:n], out[n : 2 * n], out[2 * n :]


def expo_other_kernel(a_ref, mine_ref, *refs):
    n = (len(refs) - 2) // 2
    total, weighted = expo_body(a_ref, refs[:n], refs[n : 2 * n])
    rows = weighted.shape[0]
    mine = mine_ref[...]
    refs[-2][0:1, :] = total
    refs[-2][1:2, :] = mine
    refs[-1][0:rows, :] = weighted.astype(jnp.bfloat16)
    stow(refs[-1], rows, jnp.concatenate([total, mine], axis=1))


def expo_pass(a, keys, mine=None, after=()):
    rows, width = a.shape[0] // STRIP * STRIP, a.shape[1]
    n = len(keys)
    if mine is None:
        kernel, extra = expo_mine_kernel, []
        tail = [
            jax.ShapeDtypeStruct((1, rows), jnp.float32),
            jax.ShapeDtypeStruct((rows, width), jnp.float32),
        ]
    else:
        kernel, extra = expo_other_kernel, [mine]
        tail = [
            jax.ShapeDtypeStruct((2, rows), jnp.float32),
            jax.ShapeDtypeStruct((rows + EXTRA, width), jnp.bfloat16),
        ]
    out = pl.pallas_call(
        ordered(kernel, 1 + len(extra) + n, after),
        in_specs=[VMEM] * (1 + len(extra) + n) + [ANY] * len(after),
        out_specs=[VMEM] * (n + 2),
        out_shape=[jax.ShapeDtypeStruct((rows, k.shape[0]), jnp.bfloat16) for k in keys] + tail,
        compiler_params=PARAMS,
        cost_estimate=LIGHT,
        name="expo_pass",
    )(a, *extra, *keys, *after)
    return out[:n], out[n], out[n + 1]


def turn(weighted, sent, total, matched):
    weighted = weighted + sent.astype(jnp.float32)
    return (TAU_INV * (weighted * as_column(1.0 / total) - matched)).astype(jnp.bfloat16)


def turn_first_kernel(weighted_ref, sent_ref, own_ref, matched_ref, out_ref, mine_ref, other_ref):
    rows = weighted_ref.shape[0]
    got = fetch(sent_ref, rows, 2 * rows // LINE)
    mine = own_ref[1:2, :] + got[:, 0:rows]
    mine_ref[...] = mine
    other_ref[...] = own_ref[0:1, :] + got[:, rows : 2 * rows]
    out_ref[...] = turn(weighted_ref[...], sent_ref[0:rows, :], mine, matched_ref[...])


def turn_first(weighted, sent, own, matched):
    rows, width = weighted.shape
    return pl.pallas_call(
        turn_first_kernel,
        in_specs=[VMEM] * 4,
        out_specs=[VMEM] * 3,
        out_shape=[jax.ShapeDtypeStruct((rows, width), jnp.bfloat16)]
        + [jax.ShapeDtypeStruct((1, rows), jnp.float32)] * 2,
        compiler_params=PARAMS,
        cost_estimate=LIGHT,
        name="turn_first",
    )(weighted, sent, own, matched)


def turn_last_kernel(
    weighted_ref, sent_ref, first_ref, last_ref, matched_ref, positive_ref, positive_last_ref, out_ref
):
    rows = weighted_ref.shape[0]
    last = last_ref[...]
    out_ref[0:rows, :] = turn(weighted_ref[...], sent_ref[0:rows, :], last, matched_ref[...])
    stow(
        out_ref,
        rows,
        jnp.log(jnp.concatenate([first_ref[...], last], axis=1))
        - jnp.concatenate([positive_ref[...], positive_last_ref[...]], axis=1),
    )


def turn_last(weighted, sent, first, last, matched, positive, positive_last, after):
    rows, width = weighted.shape
    return pl.pallas_call(
        ordered(turn_last_kernel, 7, after),
        in_specs=[VMEM] * 7 + [ANY] * len(after),
        out_specs=VMEM,
        out_shape=jax.ShapeDtypeStruct((rows + EXTRA, width), jnp.bfloat16),
        compiler_params=PARAMS,
        cost_estimate=LIGHT,
        name="turn_last",
    )(weighted, sent, first, last, matched, positive, positive_last, *after)


def share_kernel(*refs):
    anchors, (mine_ref, other_ref, own_ref, sent_ref) = refs[:4], refs[4:8]
    outs, last_ref = refs[8:12], refs[12]
    rows = outs[0].shape[0]
    got = fetch(sent_ref, rows, 2 * rows // LINE)
    last = own_ref[1:2, :] + got[:, 0:rows]
    last_ref[...] = last
    totals = [mine_ref[...], last, other_ref[...], own_ref[0:1, :] + got[:, rows : 2 * rows]]
    for a_ref, total, out_ref in zip(anchors, totals, outs):
        a = a_ref[0:rows, :].astype(jnp.float32)
        out_ref[...] = (a * as_column(1.0 / total)).astype(out_ref.dtype)


def share_pass(anchors, mine, other, own, sent):
    rows, width = anchors[0].shape
    out = pl.pallas_call(
        share_kernel,
        in_specs=[VMEM] * 8,
        out_specs=[VMEM] * 5,
        out_shape=[jax.ShapeDtypeStruct((rows, width), jnp.bfloat16)] * 4
        + [jax.ShapeDtypeStruct((1, rows), jnp.float32)],
        compiler_params=PARAMS,
        cost_estimate=LIGHT,
        name="share_pass",
    )(*anchors, mine, other, own, sent)
    return out[:4], out[4]


def key_kernel(*refs):
    n = len(refs) // 2
    grad = dot_cols(refs[0][...], refs[n][...])
    for e_ref, b_ref in zip(refs[1:n], refs[n + 1 : 2 * n]):
        grad += dot_cols(e_ref[...], b_ref[...])
    refs[-1][...] = (TAU_INV * grad).astype(refs[-1].dtype)


def key_pass(expos, shares, dtype, after=(), cost=LIGHT):
    rows, width = expos[0].shape[1], shares[0].shape[1]
    return pl.pallas_call(
        ordered(key_kernel, 2 * len(expos), after),
        in_specs=[VMEM] * (2 * len(expos)) + [ANY] * len(after),
        out_specs=VMEM,
        out_shape=jax.ShapeDtypeStruct((rows, width), dtype),
        compiler_params=PARAMS,
        cost_estimate=cost,
        name="key_pass",
    )(*expos, *shares, *after)


def pull(x, grad):
    scale = lax.rsqrt(jnp.sum(x * x, axis=1, keepdims=True) + 1e-06)
    unit = x * scale
    return scale * (grad - unit * jnp.sum(unit * grad, axis=1, keepdims=True))


def pull_first_kernel(x_ref, grad_ref, out_ref):
    out_ref[...] = pull(x_ref[...], grad_ref[...].astype(jnp.float32))


def pull_first(x, term, after):
    rows = term.shape[0]
    half = pl.BlockSpec((rows, x.shape[1]), lambda i: (0, 0))
    return pl.pallas_call(
        ordered(pull_first_kernel, 2, after),
        grid=(1,),
        in_specs=[half, half] + [ANY] * len(after),
        out_specs=half,
        out_shape=jax.ShapeDtypeStruct(x.shape, jnp.float32),
        compiler_params=PARAMS,
        cost_estimate=LIGHT,
        name="pull_first",
    )(x, term, *after)


def key_base_kernel(x_hbm, *refs):
    n = (len(refs) - 7) // 2
    owns, (base_ref, unit_ref, scale_ref, x_ref, sem) = refs[2 * n : 2 * n + 2], refs[2 * n + 2 :]
    load = pltpu.make_async_copy(x_hbm, x_ref, sem)
    load.start()
    grad = dot_cols(refs[0][...], refs[n][...])
    for e_ref, b_ref in zip(refs[1:n], refs[n + 1 : 2 * n]):
        grad += dot_cols(e_ref[...], b_ref[...])
    base_ref[...] = TAU_INV * grad + owns[0][...] + owns[1][...]
    load.wait()
    x = x_ref[...]
    scale = lax.rsqrt(jnp.sum(x * x, axis=1, keepdims=True) + 1e-06)
    unit_ref[...] = x * scale
    scale_ref[...] = jnp.broadcast_to(scale, scale_ref.shape)


def key_base(x, expos, shares, owns, after):
    return pl.pallas_call(
        ordered(key_base_kernel, 1 + 2 * len(expos) + 2, after),
        in_specs=[HBM] + [VMEM] * (2 * len(expos) + 2) + [ANY] * len(after),
        out_specs=[VMEM] * 3,
        out_shape=[
            jax.ShapeDtypeStruct(x.shape, jnp.float32),
            jax.ShapeDtypeStruct(x.shape, jnp.float32),
            jax.ShapeDtypeStruct((x.shape[0], 128), jnp.float32),
        ],
        scratch_shapes=[pltpu.VMEM(x.shape, jnp.float32), pltpu.SemaphoreType.DMA],
        compiler_params=PARAMS,
        cost_estimate=HEAVY,
        name="key_base",
    )(x, *expos, *shares, *owns, *after)


def pull_key_kernel(base_ref, unit_ref, scale_ref, *refs):
    terms, (out_hbm, done_ref, sems) = refs[:-3], refs[-3:]
    copies = []
    for i, start in enumerate(range(0, done_ref.shape[0], STRIP)):
        span = slice(start, start + STRIP)
        grad = base_ref[span, :]
        for ref in terms:
            grad += ref[span, :].astype(jnp.float32)
        unit = unit_ref[span, :]
        scale = scale_ref[span, 0:1]
        done_ref[span, :] = scale * (grad - unit * jnp.sum(unit * grad, axis=1, keepdims=True))
        copies.append(
            pltpu.make_async_copy(
                done_ref.at[pl.ds(start, STRIP)], out_hbm.at[pl.ds(start, STRIP)], sems.at[i]
            )
        )
        copies[-1].start()
    for copy in copies:
        copy.wait()


def pull_key(base, terms, after):
    rows, width = base[0].shape
    return pl.pallas_call(
        ordered(pull_key_kernel, 3 + len(terms), after),
        in_specs=[VMEM] * (3 + len(terms)) + [ANY] * len(after),
        out_specs=HBM,
        out_shape=jax.ShapeDtypeStruct((rows, width), jnp.float32),
        scratch_shapes=[
            pltpu.VMEM((rows, width), jnp.float32),
            pltpu.SemaphoreType.DMA((rows // STRIP,)),
        ],
        compiler_params=PARAMS,
        cost_estimate=LIGHT,
        name="pull_key",
    )(*base, *terms, *after)


def pull_rest_kernel(x_ref, grad_ref, done_ref, out_ref, loss_ref):
    del done_ref
    rows = x_ref.shape[0]
    out_ref[...] = pull(x_ref[...], grad_ref[0:rows, :].astype(jnp.float32))
    loss_ref[...] = fetch(grad_ref, rows, 2 * rows // LINE)


def pull_rest(x, term, done):
    rows = x.shape[0] // 2
    moved = pl.BlockSpec((rows, x.shape[1]), lambda i: (1, 0))
    return pl.pallas_call(
        pull_rest_kernel,
        grid=(1,),
        in_specs=[
            moved,
            pl.BlockSpec(term.shape, lambda i: (0, 0)),
            ANY,
        ],
        out_specs=[moved, pl.BlockSpec((1, 2 * rows), lambda i: (0, 0))],
        out_shape=[
            jax.ShapeDtypeStruct(x.shape, jnp.float32),
            jax.ShapeDtypeStruct((1, 2 * rows), jnp.float32),
        ],
        input_output_aliases={2: 0},
        compiler_params=PARAMS,
        cost_estimate=HEAVY,
        name="pull_rest",
    )(x, term, done)


def per_device(anchors, keys, matches):
    rows = anchors.shape[0]
    part = rows // 2
    low_0 = unit_pass(anchors, 0, part)
    low_1 = unit_pass(anchors, part, part, matches, [low_0])
    mine = [view_half(low_0), view_half(low_1)]
    k_low = unit_pass(keys, 0, rows, None, [low_1])
    pool = [k_low] + [swap(k_low, d) for d in KEY_SIDE]
    other = [swap(a, ANCHOR_SIDE) for a in mine]
    matched_0, positive_0, own_0 = match_pass(k_low, mine[0], mine[1], 0, (), FIRST)
    expo_m, total_m, weighted_m = [], [], []
    for a, after in zip(mine, ([own_0], None)):
        after = after or [total_m[0]]
        e, t, w = expo_pass(a, pool[:3], after=after)
        expo_m.append(e)
        total_m.append(t)
        weighted_m.append(w)
    rest, total_m, weighted_m = expo_rest(pool[3], mine, total_m, weighted_m)
    expo_m = [[*e, r] for e, r in zip(expo_m, rest)]
    expo_o, pair_0, weighted_o = expo_pass(other[0], pool, total_m[0], after=[total_m[1]])
    expo_o = [expo_o]
    back = [swap(weighted_o, ANCHOR_SIDE)]
    e, pair_1, weighted_o = expo_pass(other[1], pool, total_m[1], after=[pair_0])
    expo_o.append(e)
    back.append(swap(weighted_o, ANCHOR_SIDE))
    matched_1, positive_1, own_1 = match_pass(k_low, mine[1], mine[1], part, [pair_1])
    expos = expo_m + expo_o
    turn_0, mine_0, other_0 = turn_first(weighted_m[0], back[0], pair_0, matched_0)
    turned_0 = view_half(turn_0)
    shares, mine_1 = share_pass(mine + other, mine_0, other_0, pair_1, back[1])
    parts, sent = [], []
    for d in (3, 1, 2):
        parts.append(key_pass([e[d] for e in expos], shares, jnp.bfloat16, parts[-1:]))
        sent.append(swap(parts[-1], KEY_SIDE[d - 1]))
    turn_1 = turn_last(
        weighted_m[1], back[1], mine_0, mine_1, matched_1, positive_0, positive_1, parts[2:]
    )
    turned_1 = view_half(turn_1)
    base = key_base(keys, [e[0] for e in expos], shares, [own_0, own_1], [turn_1])
    anchor_grad = pull_first(anchors, turned_0, base[2:])
    anchor_grad, loss = pull_rest(anchors, turned_1, anchor_grad)
    key_grad = pull_key(base, sent, [])
    return (loss.reshape(rows), anchor_grad, key_grad)


def solution(mesh):
    placed = (P(("blk", "view"), None), P(("blk", "view"), None), P(("blk", "view"), None))
    return jax.shard_map(
        per_device,
        mesh=mesh,
        in_specs=placed,
        out_specs=(P(("blk", "view")), P(("blk", "view"), None), P(("blk", "view"), None)),
        check_vma=False,
    )
```

```python
import functools
import math

import jax
import jax.numpy as jnp
from jax import lax
from jax.experimental import pallas as pl
from jax.experimental.pallas import tpu as pltpu
from jax.sharding import PartitionSpec as P

TAU_INV = 40.0
EXP2_SCALE = TAU_INV * math.log2(math.e)
STRIP = 256
LINE = 256
EXTRA = 16
ANCHOR_SIDE = 2
KEY_SIDE = (1, 6, 7)
VMEM = pl.BlockSpec(memory_space=pltpu.VMEM)
ANY = pl.BlockSpec(memory_space=pl.ANY)
HBM = pl.BlockSpec(memory_space=pltpu.HBM)
PARAMS = pltpu.CompilerParams(vmem_limit_bytes=16 * 2**20)
HEAVY = pl.CostEstimate(flops=2**32, bytes_accessed=2**20, transcendentals=0)
FIRST = pl.CostEstimate(flops=2**32, bytes_accessed=2**20, transcendentals=0)
LIGHT = pl.CostEstimate(flops=1024, bytes_accessed=1024, transcendentals=0)


def ordered(kernel, inputs, after):
    def body(*refs):
        kernel(*refs[:inputs], *refs[inputs + len(after) :])

    return body


def gate_kernel(*refs):
    del refs


def gate(x, after):
    return pl.pallas_call(
        gate_kernel,
        in_specs=[ANY] * (1 + len(after)),
        out_specs=ANY,
        out_shape=jax.ShapeDtypeStruct(x.shape, x.dtype),
        input_output_aliases={0: 0},
        compiler_params=PARAMS,
        cost_estimate=LIGHT,
        name="gate",
    )(x, *after)


def view_half(block):
    count = lax.axis_size("view")
    route = [(i, (i + count // 2) % count) for i in range(count)]
    return lax.ppermute(block, "view", route)


def swap(block, mask):
    return lax.ppermute(block, "blk", [(i, i ^ mask) for i in range(lax.axis_size("blk"))])


def dot_rows(left, right):
    return lax.dot_general(
        left, right, (((1,), (1,)), ((), ())), preferred_element_type=jnp.float32
    )


def dot_cols(left, right):
    return lax.dot_general(
        left, right, (((0,), (0,)), ((), ())), preferred_element_type=jnp.float32
    )


def as_row(column):
    wide = jnp.broadcast_to(column, (column.shape[0], 128))
    return wide.T[0:1]


def as_column(row):
    return jnp.broadcast_to(row, (128, row.shape[1])).T[:, 0:1]


def wide(row):
    width = LINE
    return jnp.concatenate([row[:, c : c + width] for c in range(0, row.shape[1], width)], axis=0)


def flat(block):
    return jnp.concatenate([block[i : i + 1] for i in range(block.shape[0])], axis=1)


def stow(ref, start, row):
    rest = wide(row)
    parts = []
    for _ in range(3):
        part = rest.astype(jnp.bfloat16).astype(jnp.float32)
        parts.append(part)
        rest = rest - part
    parts.append(jnp.zeros((EXTRA - 3 * rest.shape[0], LINE), jnp.float32))
    ref[start : start + EXTRA, :] = jnp.concatenate(parts, axis=0).astype(jnp.bfloat16)


def fetch(ref, start, count):
    block = ref[start : start + EXTRA, :].astype(jnp.float32)
    total = block[0:count] + block[count : 2 * count] + block[2 * count : 3 * count]
    return flat(total)


def unit(x):
    return x * lax.rsqrt(jnp.sum(x * x, axis=1, keepdims=True) + 1e-06)


def unit_kernel(start, x_hbm, low_ref, x_ref, sem):
    rows = x_ref.shape[0]
    load = pltpu.make_async_copy(x_hbm.at[pl.ds(start, rows)], x_ref, sem)
    load.start()
    load.wait()
    low_ref[0:rows, :] = unit(x_ref[...]).astype(low_ref.dtype)


def unit_match_kernel(start, x_hbm, match_ref, low_ref, x_ref, sem):
    rows = x_ref.shape[0]
    load = pltpu.make_async_copy(x_hbm.at[pl.ds(start, rows)], x_ref, sem)
    load.start()
    match = match_ref[...]
    high = wide(lax.shift_right_logical(match, 5).astype(jnp.float32))
    low = wide((match & 31).astype(jnp.float32))
    fill = jnp.zeros((EXTRA - 2 * low.shape[0], LINE), jnp.float32)
    low_ref[rows : rows + EXTRA, :] = jnp.concatenate([high, low, fill], axis=0).astype(low_ref.dtype)
    load.wait()
    low_ref[0:rows, :] = unit(x_ref[...]).astype(low_ref.dtype)


def unit_pass(x, start, rows, match=None, after=()):
    width = x.shape[1]
    kernel = functools.partial(unit_kernel if match is None else unit_match_kernel, start)
    given = [x] if match is None else [x, match]
    extra = 0 if match is None else EXTRA
    return pl.pallas_call(
        ordered(kernel, len(given), after),
        in_specs=[HBM] + [VMEM] * (len(given) - 1) + [ANY] * len(after),
        out_specs=VMEM,
        out_shape=jax.ShapeDtypeStruct((rows + extra, width), jnp.bfloat16),
        scratch_shapes=[pltpu.VMEM((rows, width), jnp.float32), pltpu.SemaphoreType.DMA],
        compiler_params=PARAMS,
        cost_estimate=LIGHT,
        name="unit_pass",
    )(*given, *after)


def match_kernel(start, k_ref, a_ref, code_ref, matched_ref, positive_ref, own_ref):
    rows = k_ref.shape[0]
    part = matched_ref.shape[0]
    count = rows // LINE
    code = code_ref[part : part + EXTRA, :].astype(jnp.float32)
    match = flat(code[0:count] * 32.0 + code[count : 2 * count]).astype(jnp.int32)
    index = lax.broadcasted_iota(jnp.int32, (rows, part), 0)
    hot = (index == match[:, start : start + part]).astype(jnp.float32).astype(jnp.bfloat16)
    a = a_ref[0:part, :]
    matched = dot_cols(hot, k_ref[...])
    matched_ref[...] = matched
    score = jnp.sum(a.astype(jnp.float32) * matched, axis=1, keepdims=True)
    positive_ref[...] = as_row(score * TAU_INV)
    own_ref[...] = -TAU_INV * jnp.dot(hot, a, preferred_element_type=jnp.float32)


def match_pass(keys, anchors, code, start, after=(), cost=LIGHT):
    rows, width = keys.shape
    part = rows // 2
    return pl.pallas_call(
        ordered(functools.partial(match_kernel, start), 3, after),
        in_specs=[VMEM] * 3 + [ANY] * len(after),
        out_specs=[VMEM] * 3,
        out_shape=[
            jax.ShapeDtypeStruct((part, width), jnp.float32),
            jax.ShapeDtypeStruct((1, part), jnp.float32),
            jax.ShapeDtypeStruct((rows, width), jnp.float32),
        ],
        compiler_params=PARAMS,
        cost_estimate=cost,
        name="match_pass",
    )(keys, anchors, code, *after)


def expo_body(a_ref, keys, expos):
    rows = expos[0].shape[0]
    a = a_ref[0:rows, :]
    lanes = jnp.zeros((rows, 128), jnp.float32)
    weighted = jnp.zeros((rows, a.shape[1]), jnp.float32)
    for k_ref, e_ref in zip(keys, expos):
        for j in range(0, k_ref.shape[0], STRIP):
            k = k_ref[j : j + STRIP, :]
            expo = jnp.exp2(dot_rows(a, k) * EXP2_SCALE)
            for c in range(0, STRIP, 128):
                lanes += expo[:, c : c + 128]
            low = expo.astype(jnp.bfloat16)
            e_ref[:, j : j + STRIP] = low
            weighted += jnp.dot(low, k, preferred_element_type=jnp.float32)
    return jnp.sum(lanes.T, axis=0, keepdims=True), weighted


def expo_mine_kernel(a_ref, *refs):
    n = (len(refs) - 2) // 2
    total, weighted = expo_body(a_ref, refs[:n], refs[n : 2 * n])
    refs[-2][...] = total
    refs[-1][...] = weighted


def expo_rest_kernel(k_ref, *refs):
    n = len(refs) // 6
    for i in range(n):
        a_ref, total_ref, weighted_ref = refs[i], refs[n + i], refs[2 * n + i]
        total, weighted = expo_body(a_ref, [k_ref], [refs[3 * n + i]])
        refs[4 * n + i][...] = total_ref[...] + total
        refs[5 * n + i][...] = weighted_ref[...] + weighted


def expo_rest(key, anchors, totals, weighted):
    rows = weighted[0].shape[0]
    n = len(anchors)
    out = pl.pallas_call(
        expo_rest_kernel,
        in_specs=[VMEM] * (1 + 3 * n),
        out_specs=[VMEM] * (3 * n),
        out_shape=[jax.ShapeDtypeStruct((rows, key.shape[0]), jnp.bfloat16)] * n
        + [jax.ShapeDtypeStruct(totals[0].shape, jnp.float32)] * n
        + [jax.ShapeDtypeStruct(weighted[0].shape, jnp.float32)] * n,
        compiler_params=PARAMS,
        cost_estimate=LIGHT,
        name="expo_rest",
    )(key, *anchors, *totals, *weighted)
    return out[:n], out[n : 2 * n], out[2 * n :]


def expo_other_kernel(a_ref, mine_ref, *refs):
    n = (len(refs) - 2) // 2
    total, weighted = expo_body(a_ref, refs[:n], refs[n : 2 * n])
    rows = weighted.shape[0]
    mine = mine_ref[...]
    refs[-2][0:1, :] = total
    refs[-2][1:2, :] = mine
    refs[-1][0:rows, :] = weighted.astype(jnp.bfloat16)
    stow(refs[-1], rows, jnp.concatenate([total, mine], axis=1))


def expo_pass(a, keys, mine=None, after=()):
    rows, width = a.shape[0] // STRIP * STRIP, a.shape[1]
    n = len(keys)
    if mine is None:
        kernel, extra = expo_mine_kernel, []
        tail = [
            jax.ShapeDtypeStruct((1, rows), jnp.float32),
            jax.ShapeDtypeStruct((rows, width), jnp.float32),
        ]
    else:
        kernel, extra = expo_other_kernel, [mine]
        tail = [
            jax.ShapeDtypeStruct((2, rows), jnp.float32),
            jax.ShapeDtypeStruct((rows + EXTRA, width), jnp.bfloat16),
        ]
    out = pl.pallas_call(
        ordered(kernel, 1 + len(extra) + n, after),
        in_specs=[VMEM] * (1 + len(extra) + n) + [ANY] * len(after),
        out_specs=[VMEM] * (n + 2),
        out_shape=[jax.ShapeDtypeStruct((rows, k.shape[0]), jnp.bfloat16) for k in keys] + tail,
        compiler_params=PARAMS,
        cost_estimate=LIGHT,
        name="expo_pass",
    )(a, *extra, *keys, *after)
    return out[:n], out[n], out[n + 1]


def turn(weighted, sent, total, matched):
    weighted = weighted + sent.astype(jnp.float32)
    return (TAU_INV * (weighted * as_column(1.0 / total) - matched)).astype(jnp.bfloat16)


def turn_first_kernel(weighted_ref, sent_ref, own_ref, matched_ref, out_ref, mine_ref, other_ref):
    rows = weighted_ref.shape[0]
    got = fetch(sent_ref, rows, 2 * rows // LINE)
    mine = own_ref[1:2, :] + got[:, 0:rows]
    mine_ref[...] = mine
    other_ref[...] = own_ref[0:1, :] + got[:, rows : 2 * rows]
    out_ref[...] = turn(weighted_ref[...], sent_ref[0:rows, :], mine, matched_ref[...])


def turn_first(weighted, sent, own, matched):
    rows, width = weighted.shape
    return pl.pallas_call(
        turn_first_kernel,
        in_specs=[VMEM] * 4,
        out_specs=[VMEM] * 3,
        out_shape=[jax.ShapeDtypeStruct((rows, width), jnp.bfloat16)]
        + [jax.ShapeDtypeStruct((1, rows), jnp.float32)] * 2,
        compiler_params=PARAMS,
        cost_estimate=LIGHT,
        name="turn_first",
    )(weighted, sent, own, matched)


def turn_last_kernel(
    weighted_ref, sent_ref, first_ref, last_ref, matched_ref, positive_ref, positive_last_ref, out_ref
):
    rows = weighted_ref.shape[0]
    last = last_ref[...]
    out_ref[0:rows, :] = turn(weighted_ref[...], sent_ref[0:rows, :], last, matched_ref[...])
    stow(
        out_ref,
        rows,
        jnp.log(jnp.concatenate([first_ref[...], last], axis=1))
        - jnp.concatenate([positive_ref[...], positive_last_ref[...]], axis=1),
    )


def turn_last(weighted, sent, first, last, matched, positive, positive_last, after):
    rows, width = weighted.shape
    return pl.pallas_call(
        ordered(turn_last_kernel, 7, after),
        in_specs=[VMEM] * 7 + [ANY] * len(after),
        out_specs=VMEM,
        out_shape=jax.ShapeDtypeStruct((rows + EXTRA, width), jnp.bfloat16),
        compiler_params=PARAMS,
        cost_estimate=LIGHT,
        name="turn_last",
    )(weighted, sent, first, last, matched, positive, positive_last, *after)


def share_kernel(*refs):
    anchors, (mine_ref, other_ref, own_ref, sent_ref) = refs[:4], refs[4:8]
    outs, last_ref = refs[8:12], refs[12]
    rows = outs[0].shape[0]
    got = fetch(sent_ref, rows, 2 * rows // LINE)
    last = own_ref[1:2, :] + got[:, 0:rows]
    last_ref[...] = last
    totals = [mine_ref[...], last, other_ref[...], own_ref[0:1, :] + got[:, rows : 2 * rows]]
    for a_ref, total, out_ref in zip(anchors, totals, outs):
        a = a_ref[0:rows, :].astype(jnp.float32)
        out_ref[...] = (a * as_column(1.0 / total)).astype(out_ref.dtype)


def share_pass(anchors, mine, other, own, sent):
    rows, width = anchors[0].shape[0] // STRIP * STRIP, anchors[0].shape[1]
    out = pl.pallas_call(
        share_kernel,
        in_specs=[VMEM] * 8,
        out_specs=[VMEM] * 5,
        out_shape=[jax.ShapeDtypeStruct((rows, width), jnp.bfloat16)] * 4
        + [jax.ShapeDtypeStruct((1, rows), jnp.float32)],
        compiler_params=PARAMS,
        cost_estimate=LIGHT,
        name="share_pass",
    )(*anchors, mine, other, own, sent)
    return out[:4], out[4]


def key_kernel(*refs):
    n = len(refs) // 2
    grad = dot_cols(refs[0][...], refs[n][...])
    for e_ref, b_ref in zip(refs[1:n], refs[n + 1 : 2 * n]):
        grad += dot_cols(e_ref[...], b_ref[...])
    refs[-1][...] = (TAU_INV * grad).astype(refs[-1].dtype)


def key_pass(expos, shares, dtype, after=(), cost=LIGHT):
    rows, width = expos[0].shape[1], shares[0].shape[1]
    return pl.pallas_call(
        ordered(key_kernel, 2 * len(expos), after),
        in_specs=[VMEM] * (2 * len(expos)) + [ANY] * len(after),
        out_specs=VMEM,
        out_shape=jax.ShapeDtypeStruct((rows, width), dtype),
        compiler_params=PARAMS,
        cost_estimate=cost,
        name="key_pass",
    )(*expos, *shares, *after)


def pull(x, grad):
    scale = lax.rsqrt(jnp.sum(x * x, axis=1, keepdims=True) + 1e-06)
    unit = x * scale
    return scale * (grad - unit * jnp.sum(unit * grad, axis=1, keepdims=True))


def pull_first_kernel(x_ref, grad_ref, out_ref):
    out_ref[...] = pull(x_ref[...], grad_ref[...].astype(jnp.float32))


def pull_first(x, term, after):
    rows = term.shape[0]
    half = pl.BlockSpec((rows, x.shape[1]), lambda i: (0, 0))
    return pl.pallas_call(
        ordered(pull_first_kernel, 2, after),
        grid=(1,),
        in_specs=[half, half] + [ANY] * len(after),
        out_specs=half,
        out_shape=jax.ShapeDtypeStruct(x.shape, jnp.float32),
        compiler_params=PARAMS,
        cost_estimate=LIGHT,
        name="pull_first",
    )(x, term, *after)


def key_base_kernel(x_hbm, *refs):
    n = (len(refs) - 7) // 2
    owns, (base_ref, unit_ref, scale_ref, x_ref, sem) = refs[2 * n : 2 * n + 2], refs[2 * n + 2 :]
    load = pltpu.make_async_copy(x_hbm, x_ref, sem)
    load.start()
    grad = dot_cols(refs[0][...], refs[n][...])
    for e_ref, b_ref in zip(refs[1:n], refs[n + 1 : 2 * n]):
        grad += dot_cols(e_ref[...], b_ref[...])
    base_ref[...] = TAU_INV * grad + owns[0][...] + owns[1][...]
    load.wait()
    x = x_ref[...]
    scale = lax.rsqrt(jnp.sum(x * x, axis=1, keepdims=True) + 1e-06)
    unit_ref[...] = x * scale
    scale_ref[...] = jnp.broadcast_to(scale, scale_ref.shape)


def key_base(x, expos, shares, owns, after):
    return pl.pallas_call(
        ordered(key_base_kernel, 1 + 2 * len(expos) + 2, after),
        in_specs=[HBM] + [VMEM] * (2 * len(expos) + 2) + [ANY] * len(after),
        out_specs=[VMEM] * 3,
        out_shape=[
            jax.ShapeDtypeStruct(x.shape, jnp.float32),
            jax.ShapeDtypeStruct(x.shape, jnp.float32),
            jax.ShapeDtypeStruct((x.shape[0], 128), jnp.float32),
        ],
        scratch_shapes=[pltpu.VMEM(x.shape, jnp.float32), pltpu.SemaphoreType.DMA],
        compiler_params=PARAMS,
        cost_estimate=HEAVY,
        name="key_base",
    )(x, *expos, *shares, *owns, *after)


def pull_key_kernel(base_ref, unit_ref, scale_ref, *refs):
    terms, (out_hbm, done_ref, sems) = refs[:-3], refs[-3:]
    copies = []
    for i, start in enumerate(range(0, done_ref.shape[0], STRIP)):
        span = slice(start, start + STRIP)
        grad = base_ref[span, :]
        for ref in terms:
            grad += ref[span, :].astype(jnp.float32)
        unit = unit_ref[span, :]
        scale = scale_ref[span, 0:1]
        done_ref[span, :] = scale * (grad - unit * jnp.sum(unit * grad, axis=1, keepdims=True))
        copies.append(
            pltpu.make_async_copy(
                done_ref.at[pl.ds(start, STRIP)], out_hbm.at[pl.ds(start, STRIP)], sems.at[i]
            )
        )
        copies[-1].start()
    for copy in copies:
        copy.wait()


def pull_key(base, terms, after):
    rows, width = base[0].shape
    return pl.pallas_call(
        ordered(pull_key_kernel, 3 + len(terms), after),
        in_specs=[VMEM] * (3 + len(terms)) + [ANY] * len(after),
        out_specs=HBM,
        out_shape=jax.ShapeDtypeStruct((rows, width), jnp.float32),
        scratch_shapes=[
            pltpu.VMEM((rows, width), jnp.float32),
            pltpu.SemaphoreType.DMA((rows // STRIP,)),
        ],
        compiler_params=PARAMS,
        cost_estimate=LIGHT,
        name="pull_key",
    )(*base, *terms, *after)


def pull_rest_kernel(x_ref, grad_ref, done_ref, out_ref, loss_ref):
    del done_ref
    rows = x_ref.shape[0]
    out_ref[...] = pull(x_ref[...], grad_ref[0:rows, :].astype(jnp.float32))
    loss_ref[...] = fetch(grad_ref, rows, 2 * rows // LINE)


def pull_rest(x, term, done):
    rows = x.shape[0] // 2
    moved = pl.BlockSpec((rows, x.shape[1]), lambda i: (1, 0))
    return pl.pallas_call(
        pull_rest_kernel,
        grid=(1,),
        in_specs=[
            moved,
            pl.BlockSpec(term.shape, lambda i: (0, 0)),
            ANY,
        ],
        out_specs=[moved, pl.BlockSpec((1, 2 * rows), lambda i: (0, 0))],
        out_shape=[
            jax.ShapeDtypeStruct(x.shape, jnp.float32),
            jax.ShapeDtypeStruct((1, 2 * rows), jnp.float32),
        ],
        input_output_aliases={2: 0},
        compiler_params=PARAMS,
        cost_estimate=HEAVY,
        name="pull_rest",
    )(x, term, done)


def per_device(anchors, keys, matches):
    rows = anchors.shape[0]
    part = rows // 2
    low_0 = unit_pass(anchors, 0, part, matches)
    low_1 = unit_pass(anchors, part, part, None, [low_0])
    mine = [view_half(low_0), view_half(low_1)]
    k_low = unit_pass(keys, 0, rows, None, [low_1])
    pool = [k_low] + [swap(k_low, d) for d in KEY_SIDE]
    matched_0, positive_0, own_0 = match_pass(k_low, mine[0], mine[0], 0, (), FIRST)
    code = mine[0]
    other_0 = swap(mine[0], ANCHOR_SIDE)
    mine[1] = gate(mine[1], [own_0])
    other = [other_0, swap(mine[1], ANCHOR_SIDE)]
    expo_m, total_m, weighted_m = [], [], []
    for a, after in zip(mine, ([mine[1]], None)):
        after = after or [total_m[0]]
        e, t, w = expo_pass(a, pool[:3], after=after)
        expo_m.append(e)
        total_m.append(t)
        weighted_m.append(w)
    for i, a in enumerate(mine):
        if i:
            a = gate(a, [pair_0])
        rest, total, weighted = expo_rest(pool[3], [a], [total_m[i]], [weighted_m[i]])
        expo_m[i] = [*expo_m[i], *rest]
        total_m[i], weighted_m[i] = total[0], weighted[0]
        e, pair, weighted_o = expo_pass(other[i], pool, total_m[i])
        if i:
            expo_o.append(e)
            pair_1 = pair
        else:
            expo_o, pair_0 = [e], pair
            back = []
        back.append(swap(weighted_o, ANCHOR_SIDE))
    matched_1, positive_1, own_1 = match_pass(k_low, mine[1], code, part, [pair_1])
    expos = expo_m + expo_o
    turn_0, mine_0, other_0 = turn_first(weighted_m[0], back[0], pair_0, matched_0)
    turned_0 = view_half(turn_0)
    shares, mine_1 = share_pass(mine + other, mine_0, other_0, pair_1, back[1])
    parts, sent = [], []
    for d in (3, 1, 2):
        parts.append(key_pass([e[d] for e in expos], shares, jnp.bfloat16, parts[-1:]))
        sent.append(swap(parts[-1], KEY_SIDE[d - 1]))
    turn_1 = turn_last(
        weighted_m[1], back[1], mine_0, mine_1, matched_1, positive_0, positive_1, parts[2:]
    )
    turned_1 = view_half(turn_1)
    base = key_base(keys, [e[0] for e in expos], shares, [own_0, own_1], [turn_1])
    anchor_grad = pull_first(anchors, turned_0, base[2:])
    anchor_grad, loss = pull_rest(anchors, turned_1, anchor_grad)
    key_grad = pull_key(base, sent, [])
    return (loss.reshape(rows), anchor_grad, key_grad)


def solution(mesh):
    placed = (P(("blk", "view"), None), P(("blk", "view"), None), P(("blk", "view"), None))
    return jax.shard_map(
        per_device,
        mesh=mesh,
        in_specs=placed,
        out_specs=(P(("blk", "view")), P(("blk", "view"), None), P(("blk", "view"), None)),
        check_vma=False,
    )
```

```python
import functools
import math

import jax
import jax.numpy as jnp
from jax import lax
from jax.experimental import pallas as pl
from jax.experimental.pallas import tpu as pltpu
from jax.sharding import PartitionSpec as P

TAU_INV = 40.0
EXP2_SCALE = TAU_INV * math.log2(math.e)
STRIP = 256
LINE = 256
EXTRA = 16
ANCHOR_SIDE = 2
KEY_SIDE = (1, 6, 7)
VMEM = pl.BlockSpec(memory_space=pltpu.VMEM)
ANY = pl.BlockSpec(memory_space=pl.ANY)
HBM = pl.BlockSpec(memory_space=pltpu.HBM)
PARAMS = pltpu.CompilerParams(vmem_limit_bytes=16 * 2**20)
HEAVY = pl.CostEstimate(flops=2**32, bytes_accessed=2**20, transcendentals=0)
FIRST = pl.CostEstimate(flops=2**32, bytes_accessed=2**20, transcendentals=0)
SECOND = pl.CostEstimate(flops=2**31, bytes_accessed=2**20, transcendentals=0)
LIGHT = pl.CostEstimate(flops=1024, bytes_accessed=1024, transcendentals=0)


def ordered(kernel, inputs, after):
    def body(*refs):
        kernel(*refs[:inputs], *refs[inputs + len(after) :])

    return body


def gate_kernel(*refs):
    del refs


def gate(x, after):
    return pl.pallas_call(
        gate_kernel,
        in_specs=[ANY] * (1 + len(after)),
        out_specs=ANY,
        out_shape=jax.ShapeDtypeStruct(x.shape, x.dtype),
        input_output_aliases={0: 0},
        compiler_params=PARAMS,
        cost_estimate=LIGHT,
        name="gate",
    )(x, *after)


def view_half(block):
    count = lax.axis_size("view")
    route = [(i, (i + count // 2) % count) for i in range(count)]
    return lax.ppermute(block, "view", route)


def swap(block, mask):
    return lax.ppermute(block, "blk", [(i, i ^ mask) for i in range(lax.axis_size("blk"))])


def dot_rows(left, right):
    return lax.dot_general(
        left, right, (((1,), (1,)), ((), ())), preferred_element_type=jnp.float32
    )


def dot_cols(left, right):
    return lax.dot_general(
        left, right, (((0,), (0,)), ((), ())), preferred_element_type=jnp.float32
    )


def as_row(column):
    wide = jnp.broadcast_to(column, (column.shape[0], 128))
    return wide.T[0:1]


def as_column(row):
    return jnp.broadcast_to(row, (128, row.shape[1])).T[:, 0:1]


def wide(row):
    width = LINE
    return jnp.concatenate([row[:, c : c + width] for c in range(0, row.shape[1], width)], axis=0)


def flat(block):
    return jnp.concatenate([block[i : i + 1] for i in range(block.shape[0])], axis=1)


def stow(ref, start, row):
    rest = wide(row)
    parts = []
    for _ in range(3):
        part = rest.astype(jnp.bfloat16).astype(jnp.float32)
        parts.append(part)
        rest = rest - part
    parts.append(jnp.zeros((EXTRA - 3 * rest.shape[0], LINE), jnp.float32))
    ref[start : start + EXTRA, :] = jnp.concatenate(parts, axis=0).astype(jnp.bfloat16)


def fetch(ref, start, count):
    block = ref[start : start + EXTRA, :].astype(jnp.float32)
    total = block[0:count] + block[count : 2 * count] + block[2 * count : 3 * count]
    return flat(total)


def unit(x):
    return x * lax.rsqrt(jnp.sum(x * x, axis=1, keepdims=True) + 1e-06)


def unit_kernel(start, x_hbm, low_ref, x_ref, sem):
    rows = x_ref.shape[0]
    load = pltpu.make_async_copy(x_hbm.at[pl.ds(start, rows)], x_ref, sem)
    load.start()
    load.wait()
    low_ref[0:rows, :] = unit(x_ref[...]).astype(low_ref.dtype)


def unit_match_kernel(start, x_hbm, match_ref, low_ref, x_ref, sem):
    rows = x_ref.shape[0]
    load = pltpu.make_async_copy(x_hbm.at[pl.ds(start, rows)], x_ref, sem)
    load.start()
    match = match_ref[...]
    high = wide(lax.shift_right_logical(match, 5).astype(jnp.float32))
    low = wide((match & 31).astype(jnp.float32))
    fill = jnp.zeros((EXTRA - 2 * low.shape[0], LINE), jnp.float32)
    low_ref[rows : rows + EXTRA, :] = jnp.concatenate([high, low, fill], axis=0).astype(low_ref.dtype)
    load.wait()
    low_ref[0:rows, :] = unit(x_ref[...]).astype(low_ref.dtype)


def unit_pass(x, start, rows, match=None, after=()):
    width = x.shape[1]
    kernel = functools.partial(unit_kernel if match is None else unit_match_kernel, start)
    given = [x] if match is None else [x, match]
    extra = 0 if match is None else EXTRA
    return pl.pallas_call(
        ordered(kernel, len(given), after),
        in_specs=[HBM] + [VMEM] * (len(given) - 1) + [ANY] * len(after),
        out_specs=VMEM,
        out_shape=jax.ShapeDtypeStruct((rows + extra, width), jnp.bfloat16),
        scratch_shapes=[pltpu.VMEM((rows, width), jnp.float32), pltpu.SemaphoreType.DMA],
        compiler_params=PARAMS,
        cost_estimate=LIGHT,
        name="unit_pass",
    )(*given, *after)


def match_kernel(start, k_ref, a_ref, code_ref, matched_ref, positive_ref, own_ref):
    rows = k_ref.shape[0]
    part = matched_ref.shape[0]
    count = rows // LINE
    code = code_ref[part : part + EXTRA, :].astype(jnp.float32)
    match = flat(code[0:count] * 32.0 + code[count : 2 * count]).astype(jnp.int32)
    index = lax.broadcasted_iota(jnp.int32, (rows, part), 0)
    hot = (index == match[:, start : start + part]).astype(jnp.float32).astype(jnp.bfloat16)
    a = a_ref[0:part, :]
    matched = dot_cols(hot, k_ref[...])
    matched_ref[...] = matched
    score = jnp.sum(a.astype(jnp.float32) * matched, axis=1, keepdims=True)
    positive_ref[...] = as_row(score * TAU_INV)
    own_ref[...] = -TAU_INV * jnp.dot(hot, a, preferred_element_type=jnp.float32)


def match_pass(keys, anchors, code, start, after=(), cost=LIGHT):
    rows, width = keys.shape
    part = rows // 2
    return pl.pallas_call(
        ordered(functools.partial(match_kernel, start), 3, after),
        in_specs=[VMEM] * 3 + [ANY] * len(after),
        out_specs=[VMEM] * 3,
        out_shape=[
            jax.ShapeDtypeStruct((part, width), jnp.float32),
            jax.ShapeDtypeStruct((1, part), jnp.float32),
            jax.ShapeDtypeStruct((rows, width), jnp.float32),
        ],
        compiler_params=PARAMS,
        cost_estimate=cost,
        name="match_pass",
    )(keys, anchors, code, *after)


def expo_body(a_ref, keys, expos):
    rows = expos[0].shape[0]
    a = a_ref[0:rows, :]
    lanes = jnp.zeros((rows, 128), jnp.float32)
    weighted = jnp.zeros((rows, a.shape[1]), jnp.float32)
    for k_ref, e_ref in zip(keys, expos):
        for j in range(0, k_ref.shape[0], STRIP):
            k = k_ref[j : j + STRIP, :]
            expo = jnp.exp2(dot_rows(a, k) * EXP2_SCALE)
            for c in range(0, STRIP, 128):
                lanes += expo[:, c : c + 128]
            low = expo.astype(jnp.bfloat16)
            e_ref[:, j : j + STRIP] = low
            weighted += jnp.dot(low, k, preferred_element_type=jnp.float32)
    return jnp.sum(lanes.T, axis=0, keepdims=True), weighted


def expo_mine_kernel(a_ref, *refs):
    n = (len(refs) - 2) // 2
    total, weighted = expo_body(a_ref, refs[:n], refs[n : 2 * n])
    refs[-2][...] = total
    refs[-1][...] = weighted


def expo_close_kernel(k_ref, a_ref, o_ref, *refs):
    total_m, total_o, part_m, part_o, last_m, last_o, pair_ref, weighted_ref, sent_ref = refs
    total, weighted = expo_body(a_ref, [k_ref], [last_m])
    mine = total_m[...] + total
    weighted_ref[...] = part_m[...] + weighted
    total, weighted = expo_body(o_ref, [k_ref], [last_o])
    other = total_o[...] + total
    rows = weighted.shape[0]
    pair_ref[0:1, :] = other
    pair_ref[1:2, :] = mine
    sent_ref[0:rows, :] = (part_o[...] + weighted).astype(jnp.bfloat16)
    stow(sent_ref, rows, jnp.concatenate([other, mine], axis=1))


def expo_close(key, mine, other, total_m, total_o, part_m, part_o):
    rows, width = part_m.shape
    expo = jax.ShapeDtypeStruct((rows, key.shape[0]), jnp.bfloat16)
    return pl.pallas_call(
        expo_close_kernel,
        in_specs=[VMEM] * 7,
        out_specs=[VMEM] * 5,
        out_shape=[
            expo,
            expo,
            jax.ShapeDtypeStruct((2, rows), jnp.float32),
            jax.ShapeDtypeStruct((rows, width), jnp.float32),
            jax.ShapeDtypeStruct((rows + EXTRA, width), jnp.bfloat16),
        ],
        compiler_params=PARAMS,
        cost_estimate=LIGHT,
        name="expo_close",
    )(key, mine, other, total_m, total_o, part_m, part_o)


def expo_other_kernel(a_ref, mine_ref, *refs):
    n = (len(refs) - 2) // 2
    total, weighted = expo_body(a_ref, refs[:n], refs[n : 2 * n])
    rows = weighted.shape[0]
    mine = mine_ref[...]
    refs[-2][0:1, :] = total
    refs[-2][1:2, :] = mine
    refs[-1][0:rows, :] = weighted.astype(jnp.bfloat16)
    stow(refs[-1], rows, jnp.concatenate([total, mine], axis=1))


def expo_pass(a, keys, mine=None, after=(), cost=LIGHT):
    rows, width = a.shape[0] // STRIP * STRIP, a.shape[1]
    n = len(keys)
    if mine is None:
        kernel, extra = expo_mine_kernel, []
        tail = [
            jax.ShapeDtypeStruct((1, rows), jnp.float32),
            jax.ShapeDtypeStruct((rows, width), jnp.float32),
        ]
    else:
        kernel, extra = expo_other_kernel, [mine]
        tail = [
            jax.ShapeDtypeStruct((2, rows), jnp.float32),
            jax.ShapeDtypeStruct((rows + EXTRA, width), jnp.bfloat16),
        ]
    out = pl.pallas_call(
        ordered(kernel, 1 + len(extra) + n, after),
        in_specs=[VMEM] * (1 + len(extra) + n) + [ANY] * len(after),
        out_specs=[VMEM] * (n + 2),
        out_shape=[jax.ShapeDtypeStruct((rows, k.shape[0]), jnp.bfloat16) for k in keys] + tail,
        compiler_params=PARAMS,
        cost_estimate=cost,
        name="expo_pass",
    )(a, *extra, *keys, *after)
    return out[:n], out[n], out[n + 1]


def turn(weighted, sent, total, matched):
    weighted = weighted + sent.astype(jnp.float32)
    return (TAU_INV * (weighted * as_column(1.0 / total) - matched)).astype(jnp.bfloat16)


def turn_first_kernel(weighted_ref, sent_ref, own_ref, matched_ref, out_ref, mine_ref, other_ref):
    rows = weighted_ref.shape[0]
    got = fetch(sent_ref, rows, 2 * rows // LINE)
    mine = own_ref[1:2, :] + got[:, 0:rows]
    mine_ref[...] = mine
    other_ref[...] = own_ref[0:1, :] + got[:, rows : 2 * rows]
    out_ref[...] = turn(weighted_ref[...], sent_ref[0:rows, :], mine, matched_ref[...])


def turn_first(weighted, sent, own, matched):
    rows, width = weighted.shape
    return pl.pallas_call(
        turn_first_kernel,
        in_specs=[VMEM] * 4,
        out_specs=[VMEM] * 3,
        out_shape=[jax.ShapeDtypeStruct((rows, width), jnp.bfloat16)]
        + [jax.ShapeDtypeStruct((1, rows), jnp.float32)] * 2,
        compiler_params=PARAMS,
        cost_estimate=LIGHT,
        name="turn_first",
    )(weighted, sent, own, matched)


def turn_last_kernel(
    weighted_ref, sent_ref, first_ref, last_ref, matched_ref, positive_ref, positive_last_ref, out_ref
):
    rows = weighted_ref.shape[0]
    last = last_ref[...]
    out_ref[0:rows, :] = turn(weighted_ref[...], sent_ref[0:rows, :], last, matched_ref[...])
    stow(
        out_ref,
        rows,
        jnp.log(jnp.concatenate([first_ref[...], last], axis=1))
        - jnp.concatenate([positive_ref[...], positive_last_ref[...]], axis=1),
    )


def turn_last(weighted, sent, first, last, matched, positive, positive_last, after):
    rows, width = weighted.shape
    return pl.pallas_call(
        ordered(turn_last_kernel, 7, after),
        in_specs=[VMEM] * 7 + [ANY] * len(after),
        out_specs=VMEM,
        out_shape=jax.ShapeDtypeStruct((rows + EXTRA, width), jnp.bfloat16),
        compiler_params=PARAMS,
        cost_estimate=LIGHT,
        name="turn_last",
    )(weighted, sent, first, last, matched, positive, positive_last, *after)


def share_kernel(*refs):
    anchors, (mine_ref, other_ref, own_ref, sent_ref) = refs[:4], refs[4:8]
    outs, last_ref = refs[8:12], refs[12]
    rows = outs[0].shape[0]
    got = fetch(sent_ref, rows, 2 * rows // LINE)
    last = own_ref[1:2, :] + got[:, 0:rows]
    last_ref[...] = last
    totals = [mine_ref[...], last, other_ref[...], own_ref[0:1, :] + got[:, rows : 2 * rows]]
    for a_ref, total, out_ref in zip(anchors, totals, outs):
        a = a_ref[0:rows, :].astype(jnp.float32)
        out_ref[...] = (a * as_column(1.0 / total)).astype(out_ref.dtype)


def share_pass(anchors, mine, other, own, sent):
    rows, width = anchors[0].shape[0] // STRIP * STRIP, anchors[0].shape[1]
    out = pl.pallas_call(
        share_kernel,
        in_specs=[VMEM] * 8,
        out_specs=[VMEM] * 5,
        out_shape=[jax.ShapeDtypeStruct((rows, width), jnp.bfloat16)] * 4
        + [jax.ShapeDtypeStruct((1, rows), jnp.float32)],
        compiler_params=PARAMS,
        cost_estimate=LIGHT,
        name="share_pass",
    )(*anchors, mine, other, own, sent)
    return out[:4], out[4]


def key_kernel(*refs):
    n = len(refs) // 2
    grad = dot_cols(refs[0][...], refs[n][...])
    for e_ref, b_ref in zip(refs[1:n], refs[n + 1 : 2 * n]):
        grad += dot_cols(e_ref[...], b_ref[...])
    refs[-1][...] = (TAU_INV * grad).astype(refs[-1].dtype)


def key_pass(expos, shares, dtype, after=(), cost=LIGHT):
    rows, width = expos[0].shape[1], shares[0].shape[1]
    return pl.pallas_call(
        ordered(key_kernel, 2 * len(expos), after),
        in_specs=[VMEM] * (2 * len(expos)) + [ANY] * len(after),
        out_specs=VMEM,
        out_shape=jax.ShapeDtypeStruct((rows, width), dtype),
        compiler_params=PARAMS,
        cost_estimate=cost,
        name="key_pass",
    )(*expos, *shares, *after)


def pull(x, grad):
    scale = lax.rsqrt(jnp.sum(x * x, axis=1, keepdims=True) + 1e-06)
    unit = x * scale
    return scale * (grad - unit * jnp.sum(unit * grad, axis=1, keepdims=True))


def pull_first_kernel(x_ref, grad_ref, out_ref):
    out_ref[...] = pull(x_ref[...], grad_ref[...].astype(jnp.float32))


def pull_first(x, term, after):
    rows = term.shape[0]
    half = pl.BlockSpec((rows, x.shape[1]), lambda i: (0, 0))
    return pl.pallas_call(
        ordered(pull_first_kernel, 2, after),
        grid=(1,),
        in_specs=[half, half] + [ANY] * len(after),
        out_specs=half,
        out_shape=jax.ShapeDtypeStruct(x.shape, jnp.float32),
        compiler_params=PARAMS,
        cost_estimate=LIGHT,
        name="pull_first",
    )(x, term, *after)


def key_base_kernel(x_hbm, *refs):
    n = (len(refs) - 7) // 2
    owns, (base_ref, unit_ref, scale_ref, x_ref, sem) = refs[2 * n : 2 * n + 2], refs[2 * n + 2 :]
    load = pltpu.make_async_copy(x_hbm, x_ref, sem)
    load.start()
    grad = dot_cols(refs[0][...], refs[n][...])
    for e_ref, b_ref in zip(refs[1:n], refs[n + 1 : 2 * n]):
        grad += dot_cols(e_ref[...], b_ref[...])
    base_ref[...] = TAU_INV * grad + owns[0][...] + owns[1][...]
    load.wait()
    x = x_ref[...]
    scale = lax.rsqrt(jnp.sum(x * x, axis=1, keepdims=True) + 1e-06)
    unit_ref[...] = x * scale
    scale_ref[...] = jnp.broadcast_to(scale, scale_ref.shape)


def key_base(x, expos, shares, owns, after):
    return pl.pallas_call(
        ordered(key_base_kernel, 1 + 2 * len(expos) + 2, after),
        in_specs=[HBM] + [VMEM] * (2 * len(expos) + 2) + [ANY] * len(after),
        out_specs=[VMEM] * 3,
        out_shape=[
            jax.ShapeDtypeStruct(x.shape, jnp.float32),
            jax.ShapeDtypeStruct(x.shape, jnp.float32),
            jax.ShapeDtypeStruct((x.shape[0], 128), jnp.float32),
        ],
        scratch_shapes=[pltpu.VMEM(x.shape, jnp.float32), pltpu.SemaphoreType.DMA],
        compiler_params=PARAMS,
        cost_estimate=HEAVY,
        name="key_base",
    )(x, *expos, *shares, *owns, *after)


def pull_key_kernel(base_ref, unit_ref, scale_ref, *refs):
    terms, (out_hbm, done_ref, sems) = refs[:-3], refs[-3:]
    copies = []
    for i, start in enumerate(range(0, done_ref.shape[0], STRIP)):
        span = slice(start, start + STRIP)
        grad = base_ref[span, :]
        for ref in terms:
            grad += ref[span, :].astype(jnp.float32)
        unit = unit_ref[span, :]
        scale = scale_ref[span, 0:1]
        done_ref[span, :] = scale * (grad - unit * jnp.sum(unit * grad, axis=1, keepdims=True))
        copies.append(
            pltpu.make_async_copy(
                done_ref.at[pl.ds(start, STRIP)], out_hbm.at[pl.ds(start, STRIP)], sems.at[i]
            )
        )
        copies[-1].start()
    for copy in copies:
        copy.wait()


def pull_key(base, terms, after):
    rows, width = base[0].shape
    return pl.pallas_call(
        ordered(pull_key_kernel, 3 + len(terms), after),
        in_specs=[VMEM] * (3 + len(terms)) + [ANY] * len(after),
        out_specs=HBM,
        out_shape=jax.ShapeDtypeStruct((rows, width), jnp.float32),
        scratch_shapes=[
            pltpu.VMEM((rows, width), jnp.float32),
            pltpu.SemaphoreType.DMA((rows // STRIP,)),
        ],
        compiler_params=PARAMS,
        cost_estimate=LIGHT,
        name="pull_key",
    )(*base, *terms, *after)


def pull_rest_kernel(x_ref, grad_ref, done_ref, out_ref, loss_ref):
    del done_ref
    rows = x_ref.shape[0]
    out_ref[...] = pull(x_ref[...], grad_ref[0:rows, :].astype(jnp.float32))
    loss_ref[...] = fetch(grad_ref, rows, 2 * rows // LINE)


def pull_rest(x, term, done):
    rows = x.shape[0] // 2
    moved = pl.BlockSpec((rows, x.shape[1]), lambda i: (1, 0))
    return pl.pallas_call(
        pull_rest_kernel,
        grid=(1,),
        in_specs=[
            moved,
            pl.BlockSpec(term.shape, lambda i: (0, 0)),
            ANY,
        ],
        out_specs=[moved, pl.BlockSpec((1, 2 * rows), lambda i: (0, 0))],
        out_shape=[
            jax.ShapeDtypeStruct(x.shape, jnp.float32),
            jax.ShapeDtypeStruct((1, 2 * rows), jnp.float32),
        ],
        input_output_aliases={2: 0},
        compiler_params=PARAMS,
        cost_estimate=HEAVY,
        name="pull_rest",
    )(x, term, done)


def per_device(anchors, keys, matches):
    rows = anchors.shape[0]
    part = rows // 2
    low_0 = unit_pass(anchors, 0, part, matches)
    low_1 = unit_pass(anchors, part, part, None, [low_0])
    mine = [view_half(low_0), view_half(low_1)]
    k_low = unit_pass(keys, 0, rows, None, [low_1])
    pool = [k_low] + [swap(k_low, d) for d in KEY_SIDE]
    matched_0, positive_0, own_0 = match_pass(k_low, mine[0], mine[0], 0, (), FIRST)
    code = mine[0]
    other_0 = swap(mine[0], ANCHOR_SIDE)
    mine[1] = gate(mine[1], [own_0])
    other = [other_0, swap(mine[1], ANCHOR_SIDE)]
    expo_m0, total_m, part_m = expo_pass(mine[0], pool[:3], after=[mine[1]])
    expo_o0, total_o, part_o = expo_pass(other[0], pool[:3], after=[total_m], cost=SECOND)
    last_m, last_o, pair_0, part_m, sent_0 = expo_close(
        pool[3], mine[0], other[0], total_m, total_o, part_m, part_o
    )
    back = [swap(sent_0, ANCHOR_SIDE)]
    expo_m1, total_m1, part_m1 = expo_pass(mine[1], pool, after=[pair_0])
    weighted_m = [part_m, part_m1]
    expo_o1, pair_1, sent_1 = expo_pass(other[1], pool, total_m1)
    back.append(swap(sent_1, ANCHOR_SIDE))
    expo_m = [[*expo_m0, last_m], expo_m1]
    expo_o = [[*expo_o0, last_o], expo_o1]
    matched_1, positive_1, own_1 = match_pass(k_low, mine[1], code, part, [pair_1])
    expos = expo_m + expo_o
    turn_0, mine_0, other_0 = turn_first(weighted_m[0], back[0], pair_0, matched_0)
    turned_0 = view_half(turn_0)
    shares, mine_1 = share_pass(mine + other, mine_0, other_0, pair_1, back[1])
    parts, sent = [], []
    for d in (3, 1, 2):
        parts.append(key_pass([e[d] for e in expos], shares, jnp.bfloat16, parts[-1:]))
        sent.append(swap(parts[-1], KEY_SIDE[d - 1]))
    turn_1 = turn_last(
        weighted_m[1], back[1], mine_0, mine_1, matched_1, positive_0, positive_1, parts[2:]
    )
    turned_1 = view_half(turn_1)
    base = key_base(keys, [e[0] for e in expos], shares, [own_0, own_1], [turn_1])
    anchor_grad = pull_first(anchors, turned_0, base[2:])
    anchor_grad, loss = pull_rest(anchors, turned_1, anchor_grad)
    key_grad = pull_key(base, sent, [])
    return (loss.reshape(rows), anchor_grad, key_grad)


def solution(mesh):
    placed = (P(("blk", "view"), None), P(("blk", "view"), None), P(("blk", "view"), None))
    return jax.shard_map(
        per_device,
        mesh=mesh,
        in_specs=placed,
        out_specs=(P(("blk", "view")), P(("blk", "view"), None), P(("blk", "view"), None)),
        check_vma=False,
    )
```
